32 devices in a mesh: groups: 2 (over x), expert: 8 (over z, y), hidden: 2 (over core).
Axes of the slice: x: 2, y: 2, z: 4, core: 2. Of those that a mesh axis runs over, the one named last changes fastest.
Arguments:
- tokens: bfloat16 [4096, 768], P(('groups', 'expert', 'hidden')), parts along dimension 0, may hold values from -6 to 6
- grad_out: bfloat16 [4096, 768], P(('groups', 'expert', 'hidden')), parts along dimension 0, may hold values from -24 to 24
- probs: float32 [4096, 8], P(('groups', 'expert', 'hidden')), parts along dimension 0, may hold values from 0 to 1, as said below
- choices: int32 [16, 256], P('groups'), parts along dimension 0, may hold values from 0 to 2047, as said below
- w_in: bfloat16 [8, 768, 3072], P('expert', None, 'hidden'), may hold values from -0.21875 to 0.21875
- w_out: bfloat16 [8, 3072, 768], P('expert', 'hidden'), may hold values from -0.109375 to 0.109375
- router: float32 [768, 8], replicated, may hold values from -0.0546875 to 0.0546875
Outputs:
- grad_tokens: bfloat16 [4096, 768], P(('groups', 'expert', 'hidden')), parts along dimension 0
- grad_w_in: bfloat16 [16, 768, 3072], P(('groups', 'expert'), None, 'hidden'), parts along dimension 0
- grad_w_out: bfloat16 [16, 3072, 768], P(('groups', 'expert'), 'hidden'), parts along dimension 0
- grad_logits: float32 [4096, 8], P(('groups', 'expert', 'hidden')), parts along dimension 0
The draws below stay inside these ranges and needn't reach their ends.
There are 2 independent parts, one for each index of `groups`. The reference program is written for one: setup_inputs(seed, part) draws one part's arguments, and reference() takes and returns one part's arrays. A program takes and returns all parts, laid end to end along the dimension named above; an argument that names none is the same for every part. Nothing has to cross between parts.
Inputs may be any that keep to these rules, and one draw needn't show every extreme that they name: `choices`: every row holds 256 distinct token indices in ascending order. At most 32 entries of one row lie among the tokens of one device (indices k * 128 to (k + 1) * 128 - 1), and every row has exactly 32 on some device. `probs`: each row is positive and sums to one.
All inputs are finite; a program needn't handle non-finite values.
Results may differ from the reference program's by a relative error of at most 0.0065.
Values may be sent and summed in bfloat16 or wider, within the bound.
A program may use at most 64 MiB of HBM per device.

```python
import math
import jax
import jax.numpy as jnp
from jax import lax

D = 768
FF = 3072
TOK_DEV = 128
EXPERTS = 8
OWNERS = 16
TOKENS = 2048
CAP = 256
SLOT = 32


def draw_probs(key, part):
    key = jax.random.fold_in(key, 5)
    key_logits = jax.random.fold_in(key, 0)
    logits = 1.5 * jax.random.normal(key_logits, (TOKENS, EXPERTS), jnp.float32)
    return jax.nn.softmax(logits, axis=-1)


def draw_choices(key, part):
    key = jax.random.fold_in(key, 11)
    key_perm, key_count, key_pick = jax.random.split(key, 3)
    half = OWNERS // 2
    shuffled = jax.random.permutation(key_perm, OWNERS)
    popular = shuffled[:half]
    quiet = shuffled[half:]
    heavy = SLOT - jax.random.randint(key_count, (EXPERTS, half), 0, SLOT // 4 + 1)
    heavy = heavy.at[:, 0].set(SLOT)
    counts = jnp.zeros((EXPERTS, OWNERS), jnp.int32)
    counts = counts.at[:, popular].set(heavy).at[:, quiet].set(SLOT - heavy)
    scores = jax.random.randint(key_pick, (EXPERTS, OWNERS, TOK_DEV), 0, 1 << 20)
    scores = scores * TOK_DEV + jnp.arange(TOK_DEV, dtype=jnp.int32)
    picked = jnp.argsort(scores, axis=-1)[:, :, :SLOT].astype(jnp.int32)
    place = jnp.arange(SLOT, dtype=jnp.int32)
    usable = place < counts[:, :, None]
    local_ids = jnp.sort(jnp.where(usable, picked, TOK_DEV), axis=-1)
    global_ids = local_ids + jnp.arange(OWNERS, dtype=jnp.int32)[:, None] * TOK_DEV
    flat_ids = global_ids.reshape(EXPERTS, OWNERS * SLOT)
    order_keys = jnp.where(usable, 0, OWNERS * SLOT).reshape(EXPERTS, OWNERS * SLOT)
    order_keys = order_keys + jnp.arange(OWNERS * SLOT, dtype=jnp.int32)
    ordering = jnp.argsort(order_keys, axis=-1)[:, :CAP]
    return jnp.take_along_axis(flat_ids, ordering, axis=-1).astype(jnp.int32)


def block_levels(key, extent, pieces, low, largest):
    factor_of = 1.0
    for position, shards_of in pieces:
        draws = jax.random.uniform(jax.random.fold_in(jax.random.fold_in(key, 6), position), (shards_of,), jnp.float32, low / len(pieces), largest / len(pieces))
        factor_of = factor_of * jnp.repeat(jnp.exp(draws), extent[position] // shards_of).reshape((-1,) + (1,) * (len(extent) - 1 - position))
    return factor_of


def normal_values(rng, shape, width, reach, shards=(), held_as=jnp.bfloat16):
    array = width * jax.random.normal(rng, shape, jnp.float32)
    if shards:
        array = array * block_levels(rng, shape, shards, -0.22, 0.18)
    return jnp.clip(array, -reach, reach).astype(held_as)


def setup_inputs(seed: int = 0, part: int = 0) -> dict:
    streams_of = jax.random.split(jax.random.key(seed), 8)
    part_splits = jax.random.split(jax.random.fold_in(streams_of[7], part), 8)
    tokens = normal_values(part_splits[0], (TOKENS, D), 1.0, 6.0, ((0, 16),))
    grad_out = normal_values(part_splits[1], (TOKENS, D), 4.0, 24.0, ((0, 16),))
    probs = draw_probs(jax.random.fold_in(jax.random.fold_in(streams_of[7], part), 71), part)
    choices = draw_choices(jax.random.fold_in(jax.random.fold_in(streams_of[7], part), 71), part)
    w_in = normal_values(streams_of[4], (EXPERTS, D, FF), D ** -0.5, 0.21875, ((0, 8), (2, 2)))
    w_out = normal_values(streams_of[5], (EXPERTS, FF, D), FF ** -0.5, 0.109375, ((0, 8), (1, 2)))
    router = normal_values(streams_of[6], (D, EXPERTS), (16 * D) ** -0.5, 0.0546875, (), jnp.float32)
    return {"tokens": tokens, "grad_out": grad_out, "probs": probs, "choices": choices, "w_in": w_in, "w_out": w_out, "router": router}


gelu_scale = math.sqrt(2.0 / math.pi)
cubic_coef = 0.044715

def gelu_parts(inputs):
    tanh_value = jnp.tanh(gelu_scale * (inputs + cubic_coef * inputs * inputs * inputs))
    gelu_value = 0.5 * inputs * (1.0 + tanh_value)
    gelu_slope = 0.5 * (1.0 + tanh_value) + 0.5 * inputs * (1.0 - tanh_value * tanh_value) * gelu_scale * (1.0 + 3.0 * cubic_coef * inputs * inputs)
    return (gelu_value, gelu_slope)

def reference(tokens, grad_out, probs, choices, w_in, w_out, router):

    def one_expert(operands):
        w_first, w_second, token_ids, column = operands
        token_rows = tokens[token_ids]
        grad_rows = grad_out[token_ids]
        gate_rows = probs[token_ids, column].astype(jnp.bfloat16)
        pre_act = jnp.dot(token_rows, w_first, preferred_element_type=jnp.float32)
        gelu_value, gelu_slope = gelu_parts(pre_act)
        activation = gelu_value.astype(jnp.bfloat16)
        branch_out = jnp.dot(activation, w_second, preferred_element_type=jnp.float32)
        gate_grad = lax.optimization_barrier(jnp.sum(grad_rows.astype(jnp.float32) * branch_out, axis=-1))
        scaled_grad = (gate_rows.astype(jnp.float32)[:, None] * grad_rows.astype(jnp.float32)).astype(jnp.bfloat16)
        act_grad = jnp.dot(scaled_grad, w_second.T, preferred_element_type=jnp.float32)
        pre_grad = (act_grad * gelu_slope).astype(jnp.bfloat16)
        grad_second = jnp.dot(activation.T, scaled_grad, preferred_element_type=jnp.float32).astype(jnp.bfloat16)
        grad_first = jnp.dot(token_rows.T, pre_grad, preferred_element_type=jnp.float32).astype(jnp.bfloat16)
        input_part = jnp.dot(pre_grad, w_first.T, preferred_element_type=jnp.float32)
        return (grad_first, grad_second, input_part, gate_grad)
    columns = jnp.arange(EXPERTS, dtype=jnp.int32)
    grad_w_in, grad_w_out, input_parts, gate_grad = lax.map(one_expert, (w_in, w_out, choices, columns))
    moe_grad = jnp.zeros((TOKENS, D), jnp.float32).at[choices.reshape(-1)].add(input_parts.reshape(-1, D))
    score_grad = jnp.zeros((TOKENS, EXPERTS), jnp.float32).at[choices, columns[:, None]].add(gate_grad)
    grad_logits = probs * (score_grad - lax.optimization_barrier(jnp.sum(probs * score_grad, axis=-1, keepdims=True)))
    router_part = jnp.dot(grad_logits, router.T, precision=lax.Precision.HIGHEST, preferred_element_type=jnp.float32)
    grad_tokens = (moe_grad + router_part).astype(jnp.bfloat16)
    return (grad_tokens, grad_w_in, grad_w_out, grad_logits)
```

```python
import functools
import math

import jax
import jax.numpy as jnp
from jax import lax
from jax.experimental import pallas as pl
from jax.experimental.pallas import tpu as pltpu
from jax.sharding import PartitionSpec as P

gelu_scale = math.sqrt(2.0 / math.pi)
cubic_coef = 0.044715


def gelu_parts(inputs):
    tanh_value = jnp.tanh(gelu_scale * (inputs + cubic_coef * inputs * inputs * inputs))
    gelu_value = 0.5 * inputs * (1.0 + tanh_value)
    gelu_slope = 0.5 * (1.0 + tanh_value) + 0.5 * inputs * (
        1.0 - tanh_value * tanh_value
    ) * gelu_scale * (1.0 + 3.0 * cubic_coef * inputs * inputs)
    return (gelu_value, gelu_slope)


def expert_pass(token_rows, grad_rows, gate_rows, w_first, w_second):
    leading = token_rows.shape[:-1]
    width = token_rows.shape[-1]
    flat_tokens = token_rows.reshape(-1, width)
    flat_grads = grad_rows.reshape(-1, width)
    flat_gates = gate_rows.reshape(-1)
    pre_act = jnp.dot(flat_tokens, w_first, preferred_element_type=jnp.float32)
    gelu_value, gelu_slope = gelu_parts(pre_act)
    activation = gelu_value.astype(jnp.bfloat16)
    branch_out = jnp.dot(activation, w_second, preferred_element_type=jnp.float32)
    gate_grad = jnp.sum(flat_grads.astype(jnp.float32) * branch_out, axis=-1)
    scaled_grad = (flat_gates.astype(jnp.float32)[:, None] * flat_grads.astype(jnp.float32)).astype(
        jnp.bfloat16
    )
    act_grad = lax.dot_general(
        scaled_grad, w_second, (((1,), (1,)), ((), ())), preferred_element_type=jnp.float32
    )
    pre_grad = (act_grad * gelu_slope).astype(jnp.bfloat16)
    input_part = lax.dot_general(
        pre_grad, w_first, (((1,), (1,)), ((), ())), preferred_element_type=jnp.float32
    )
    hidden_width = w_first.shape[1]
    return (
        input_part.reshape(leading + (width,)),
        gate_grad.reshape(leading),
        token_rows,
        activation.reshape(leading + (hidden_width,)),
        scaled_grad.reshape(leading + (width,)),
        pre_grad.reshape(leading + (hidden_width,)),
    )


def general_body(tokens, grad_out, probs, choices, w_in, w_out, router):
    tok_dev, width = tokens.shape
    experts, capacity = choices.shape
    expert_count = lax.axis_size("expert")
    hidden_count = lax.axis_size("hidden")
    owner_count = expert_count * hidden_count
    slot_count = 2 * capacity // owner_count
    slot_total = experts * slot_count
    my_owner = lax.axis_index("expert") * hidden_count + lax.axis_index("hidden")
    w_first = w_in[0]
    w_second = w_out[0]
    owners_of = choices // tok_dev
    before = jnp.sum((owners_of < my_owner).astype(jnp.int32), axis=1)
    mine_count = jnp.sum((owners_of == my_owner).astype(jnp.int32), axis=1)
    slot_rank = lax.broadcasted_iota(jnp.int32, (experts, slot_count), 1)
    position = before[:, None] + slot_rank
    pick_mask = (
        lax.broadcasted_iota(jnp.int32, (experts, slot_count, capacity), 2) == position[:, :, None]
    )
    picked = jnp.sum(jnp.where(pick_mask, choices[:, None, :], 0), axis=2)
    slot_token = jnp.where(
        slot_rank < mine_count[:, None], picked - my_owner * tok_dev, tok_dev
    ).reshape(-1)
    slot_expert = lax.broadcasted_iota(jnp.int32, (experts, slot_count), 0).reshape(-1)
    selector = slot_token[:, None] == lax.broadcasted_iota(jnp.int32, (slot_total, tok_dev), 1)
    select_half = selector.astype(jnp.bfloat16)
    select_full = selector.astype(jnp.float32)
    expert_mask = slot_expert[:, None] == lax.broadcasted_iota(jnp.int32, (slot_total, experts), 1)
    stacked = jnp.concatenate([tokens, grad_out], axis=1)
    picked_rows = jnp.dot(select_half, stacked, preferred_element_type=jnp.float32).astype(
        jnp.bfloat16
    )
    send_tokens = picked_rows[:, :width].reshape(experts, slot_count, width)
    send_grads = picked_rows[:, width:].reshape(experts, slot_count, width)
    prob_rows = jnp.dot(
        select_full, probs, precision=lax.Precision.HIGHEST, preferred_element_type=jnp.float32
    )
    send_gates = (
        jnp.sum(jnp.where(expert_mask, prob_rows, 0.0), axis=1)
        .astype(jnp.bfloat16)
        .reshape(experts, slot_count)
    )

    def doubled(array):
        spread = jnp.broadcast_to(array[:, None], (experts, hidden_count) + array.shape[1:])
        return spread.reshape((experts * hidden_count,) + array.shape[1:])

    results = expert_pass(
        lax.all_to_all(
            doubled(send_tokens), ("expert", "hidden"), split_axis=0, concat_axis=0, tiled=True
        ),
        lax.all_to_all(
            doubled(send_grads), ("expert", "hidden"), split_axis=0, concat_axis=0, tiled=True
        ),
        lax.all_to_all(
            doubled(send_gates), ("expert", "hidden"), split_axis=0, concat_axis=0, tiled=True
        ),
        w_first,
        w_second,
    )
    input_part, gate_part, token_rows, activation, scaled_grad, pre_grad = results
    hidden_width = w_first.shape[1]
    grad_first = lax.dot_general(
        token_rows.reshape(-1, width),
        pre_grad.reshape(-1, hidden_width),
        (((0,), (0,)), ((), ())),
        preferred_element_type=jnp.float32,
    )
    grad_second = lax.dot_general(
        activation.reshape(-1, hidden_width),
        scaled_grad.reshape(-1, width),
        (((0,), (0,)), ((), ())),
        preferred_element_type=jnp.float32,
    )
    grad_w_in = grad_first.astype(jnp.bfloat16)[None]
    grad_w_out = grad_second.astype(jnp.bfloat16)[None]
    back_rows, back_gates = (
        lax.all_to_all(input_part, ("expert", "hidden"), split_axis=0, concat_axis=0, tiled=True),
        lax.all_to_all(gate_part, ("expert", "hidden"), split_axis=0, concat_axis=0, tiled=True),
    )
    rows_back = jnp.sum(back_rows.reshape(experts, hidden_count, slot_count, width), axis=1)
    gates_back = jnp.sum(back_gates.reshape(experts, hidden_count, slot_count), axis=1)
    moe_grad = lax.dot_general(
        select_full,
        rows_back.reshape(slot_total, width),
        (((0,), (0,)), ((), ())),
        precision=lax.Precision.HIGHEST,
        preferred_element_type=jnp.float32,
    )
    gate_table = jnp.where(expert_mask, gates_back.reshape(-1)[:, None], 0.0)
    score_grad = lax.dot_general(
        select_full,
        gate_table,
        (((0,), (0,)), ((), ())),
        precision=lax.Precision.HIGHEST,
        preferred_element_type=jnp.float32,
    )
    grad_logits = probs * (score_grad - jnp.sum(probs * score_grad, axis=-1, keepdims=True))
    router_part = lax.dot_general(
        grad_logits,
        router,
        (((1,), (1,)), ((), ())),
        precision=lax.Precision.HIGHEST,
        preferred_element_type=jnp.float32,
    )
    grad_tokens = (moe_grad + router_part).astype(jnp.bfloat16)
    return (grad_tokens, grad_w_in, grad_w_out, grad_logits)


MESH = pl.DeviceIdType.MESH


def matmul(a, b, contract):
    return lax.dot_general(a, b, (contract, ((), ())), preferred_element_type=jnp.float32)


NN = ((1,), (0,))
NT = ((1,), (1,))
TN = ((0,), (0,))


def fused_kernel(
    experts,
    slots,
    tile,
    tokens_ref,
    grads_ref,
    probs_ref,
    choices_ref,
    router_ref,
    w_in_hbm,
    w_out_hbm,
    grad_tokens_ref,
    grad_logits_ref,
    grad_w_in_hbm,
    grad_w_out_hbm,
    w_in_ref,
    w_out_ref,
    select_ref,
    send_ref,
    rows_ref,
    scaled_ref,
    act_ref,
    pre_grad_ref,
    part_ref,
    pair_ref,
    ret_ref,
    back_ref,
    first_ref,
    second_ref,
    weight_sem,
    go_send,
    go_recv,
    fwd_send,
    fwd_recv,
    pair_send,
    pair_recv,
    ret_send,
    ret_recv,
    first_sem,
    second_sem,
):
    tok_dev, width = tokens_ref.shape
    hidden = w_in_ref.shape[1]
    half = experts // 2
    chunk = half * slots
    me = lax.axis_index("expert")
    core = lax.axis_index("hidden")
    base = (me * 2 + core) * tok_dev
    side = me // half
    place = me % half

    def target(step):
        where = side if step < half else 1 - side
        return where * half + (place + step) % half

    def source(step):
        where = side if step < half else 1 - side
        return where * half + (place + 2 * half - step) % half

    def direct_row(step):
        return (step // half) * 2 * chunk + (step % half) * slots

    sibling = {"hidden": 1 - core}
    barrier = pltpu.get_barrier_semaphore()
    for step in range(1, experts):
        pl.semaphore_signal(
            barrier, inc=1, device_id={"expert": target(step)}, device_id_type=MESH
        )
    pl.semaphore_signal(barrier, inc=1, device_id=sibling, device_id_type=MESH)
    load_in = pltpu.make_async_copy(w_in_hbm.at[0], w_in_ref, weight_sem.at[0])
    load_out = pltpu.make_async_copy(w_out_hbm.at[0], w_out_ref, weight_sem.at[1])
    load_in.start()
    load_out.start()

    def go_copy(step):
        return pltpu.make_async_remote_copy(
            src_ref=send_ref.at[pl.ds(step * slots, slots)],
            dst_ref=rows_ref.at[pl.ds(direct_row(step), slots)],
            send_sem=go_send.at[step],
            recv_sem=go_recv.at[step],
            device_id={"expert": target(step)},
            device_id_type=MESH,
        )

    def fwd_copy(step):
        return pltpu.make_async_remote_copy(
            src_ref=rows_ref.at[pl.ds(direct_row(step), slots)],
            dst_ref=rows_ref.at[pl.ds(direct_row(step) + chunk, slots)],
            send_sem=fwd_send.at[step],
            recv_sem=fwd_recv.at[step],
            device_id=sibling,
            device_id_type=MESH,
        )

    def pair_copy(part):
        return pltpu.make_async_remote_copy(
            src_ref=part_ref.at[part, pl.ds(chunk, chunk)],
            dst_ref=pair_ref.at[part],
            send_sem=pair_send.at[part],
            recv_sem=pair_recv.at[part],
            device_id=sibling,
            device_id_type=MESH,
        )

    def ret_copy(step):
        return pltpu.make_async_remote_copy(
            src_ref=ret_ref.at[pl.ds(step * slots, slots)],
            dst_ref=back_ref.at[pl.ds(step * slots, slots)],
            send_sem=ret_send.at[step],
            recv_sem=ret_recv.at[step],
            device_id={"expert": source(step)},
            device_id_type=MESH,
        )

    probs = probs_ref[...]
    probs_half = probs.astype(jnp.bfloat16)
    capacity = choices_ref.shape[1]
    rank_gap = lax.broadcasted_iota(jnp.int32, (slots, capacity), 1) - lax.broadcasted_iota(
        jnp.int32, (slots, capacity), 0
    )
    rank_gap = rank_gap.astype(jnp.float32)
    token_id = lax.broadcasted_iota(jnp.int32, (tok_dev, capacity), 0) + base
    column = lax.broadcasted_iota(jnp.int32, (slots, experts), 1)

    def select(part):
        for step in range(part * half, (part + 1) * half):
            row = choices_ref[pl.ds(target(step), 1), :]
            before = jnp.sum(jnp.where(row < base, 1.0, 0.0), axis=1, keepdims=True)
            pick = jnp.where(rank_gap == before, 1.0, 0.0).astype(jnp.bfloat16)
            equal = jnp.where(token_id == row, 1.0, 0.0).astype(jnp.bfloat16)
            select_ref[pl.ds(step * slots, slots), :] = matmul(pick, equal, NT).astype(jnp.bfloat16)
        chosen = select_ref[pl.ds(part * chunk, chunk), :]
        token_rows = matmul(chosen, tokens_ref[...], NN).astype(jnp.bfloat16)
        grad_rows = matmul(chosen, grads_ref[...], NN).astype(jnp.bfloat16)
        gates = matmul(chosen, probs_half, NN)
        for index in range(half):
            step = part * half + index
            mine = slice(index * slots, (index + 1) * slots)
            gate = jnp.sum(
                jnp.where(column == target(step), gates[mine], 0.0), axis=1, keepdims=True
            )
            gate = jnp.broadcast_to(gate, (slots, 128)).astype(jnp.bfloat16)
            ref = rows_ref if step == 0 else send_ref
            at = pl.ds(step * slots, slots)
            ref[at, :width] = token_rows[mine]
            ref[at, width : 2 * width] = grad_rows[mine]
            ref[at, 2 * width :] = gate

    select(1)
    pl.semaphore_wait(barrier, experts)
    for step in range(half, experts):
        go_copy(step).start()
    select(0)
    for step in range(1, half):
        go_copy(step).start()

    def forward(part):
        for step in range(part * half, (part + 1) * half):
            if step:
                go_copy(step).wait_recv()
            fwd_copy(step).start()

    def compute(part):
        for step in range(part * half, (part + 1) * half):
            fwd_copy(step).wait_recv()
        rows = pl.ds(part * 2 * chunk, 2 * chunk)
        gate = rows_ref[rows, 2 * width :].astype(jnp.float32)
        wide_gate = jnp.concatenate([gate] * (width // 128), axis=1)
        scaled_ref[rows, :] = (
            wide_gate * rows_ref[rows, width : 2 * width].astype(jnp.float32)
        ).astype(jnp.bfloat16)
        part_ref[part] = jnp.zeros(part_ref.shape[1:], jnp.float32)

        def step_tile(index, carry):
            at = pl.ds(pl.multiple_of(index * tile, tile), tile)
            w_first = w_in_ref[:, at]
            w_second = w_out_ref[at, :]
            pre_act = matmul(rows_ref[rows, :width], w_first, NN)
            raw_grad = matmul(rows_ref[rows, width : 2 * width], w_second, NT)
            gelu_value, gelu_slope = gelu_parts(pre_act)
            act = gelu_value.astype(jnp.bfloat16)
            act_ref[rows, at] = act
            product = act.astype(jnp.float32) * raw_grad
            gate_tile = jnp.concatenate([gate] * (tile // 128), axis=1)
            pre_grad = (gate_tile * raw_grad * gelu_slope).astype(jnp.bfloat16)
            pre_grad_ref[rows, at] = pre_grad
            part_ref[part, :, :width] += matmul(pre_grad, w_first, NT)
            total = product[:, :128]
            for lane in range(128, tile, 128):
                total = total + product[:, lane : lane + 128]
            part_ref[part, :, width:] += total
            return carry

        lax.fori_loop(0, hidden // tile, step_tile, 0)
        pair_copy(part).start()

    lane = lax.broadcasted_iota(jnp.int32, (chunk, 128), 1)

    def give_back(part):
        pair_copy(part).wait_recv()
        total = part_ref[part, :chunk, :] + pair_ref[part]
        gate_grad = jnp.sum(total[:, width:], axis=1, keepdims=True)
        high = gate_grad.astype(jnp.bfloat16).astype(jnp.float32)
        low = gate_grad - high
        coded = jnp.where(lane == me, high, jnp.where(lane == me + experts, low, 0.0))
        values = total[:, :width].astype(jnp.bfloat16)
        coded = coded.astype(jnp.bfloat16)
        for index in range(half):
            step = part * half + index
            mine = slice(index * slots, (index + 1) * slots)
            ref = ret_ref if step else back_ref
            ref[pl.ds(step * slots, slots), :width] = values[mine]
            ref[pl.ds(step * slots, slots), width:] = coded[mine]
            if step:
                ret_copy(step).start()

    first_rows = 256
    second_rows = 256

    def first_out(index):
        at = pl.ds(pl.multiple_of(index * first_rows, first_rows), first_rows)
        return pltpu.make_async_copy(
            first_ref.at[at], grad_w_in_hbm.at[0, at], first_sem.at[index]
        )

    def second_out(index):
        at = pl.ds(pl.multiple_of(index * second_rows, second_rows), second_rows)
        return pltpu.make_async_copy(
            second_ref.at[at], grad_w_out_hbm.at[0, at], second_sem.at[index]
        )

    def first_grad(index, carry):
        at = pl.ds(pl.multiple_of(index * first_rows, first_rows), first_rows)
        first_ref[at, :] = matmul(rows_ref[:, at], pre_grad_ref[...], TN).astype(jnp.bfloat16)
        first_out(index).start()
        return carry

    def second_grad(index, carry):
        at = pl.ds(pl.multiple_of(index * second_rows, second_rows), second_rows)
        second_ref[at, :] = matmul(act_ref[:, at], scaled_ref[...], TN).astype(jnp.bfloat16)
        second_out(index).start()
        return carry

    forward(0)
    load_in.wait()
    load_out.wait()
    compute(0)
    forward(1)
    give_back(0)
    compute(1)
    first_count = width // first_rows
    second_count = hidden // second_rows
    lax.fori_loop(0, 1, first_grad, 0)
    give_back(1)
    lax.fori_loop(1, first_count, first_grad, 0)
    lax.fori_loop(0, second_count, second_grad, 0)

    for step in range(1, experts):
        ret_copy(step).wait_recv()
    summed = matmul(select_ref[...], back_ref[...], TN)
    score_grad = (
        summed[:, width : width + experts] + summed[:, width + experts : width + 2 * experts]
    )
    grad_logits = probs * (score_grad - jnp.sum(probs * score_grad, axis=-1, keepdims=True))
    grad_logits_ref[...] = grad_logits
    router_part = lax.dot_general(
        grad_logits,
        router_ref[...],
        (NT, ((), ())),
        precision=lax.Precision.HIGHEST,
        preferred_element_type=jnp.float32,
    )
    grad_tokens_ref[...] = (summed[:, :width] + router_part).astype(jnp.bfloat16)

    for step in range(1, experts):
        go_copy(step).wait_send()
        ret_copy(step).wait_send()
    for step in range(experts):
        fwd_copy(step).wait_send()
    for part in range(2):
        pair_copy(part).wait_send()
    for index in range(first_count):
        first_out(index).wait()
    for index in range(second_count):
        second_out(index).wait()


def fused_body(tokens, grad_out, probs, choices, w_in, w_out, router):
    tok_dev, width = tokens.shape
    experts, capacity = choices.shape
    hidden = w_in.shape[2]
    slots = 2 * capacity // (experts * lax.axis_size("hidden"))
    total = experts * slots
    half_type = jnp.bfloat16
    vmem = pl.BlockSpec(memory_space=pltpu.VMEM)
    hbm = pl.BlockSpec(memory_space=pl.ANY)
    dma = pltpu.SemaphoreType.DMA
    grad_tokens, grad_logits, grad_w_in, grad_w_out = pl.pallas_call(
        functools.partial(fused_kernel, experts, slots, 512),
        out_shape=(
            jax.ShapeDtypeStruct(tokens.shape, half_type),
            jax.ShapeDtypeStruct(probs.shape, jnp.float32),
            jax.ShapeDtypeStruct(w_in.shape, half_type),
            jax.ShapeDtypeStruct(w_out.shape, half_type),
        ),
        in_specs=[vmem, vmem, vmem, vmem, vmem, hbm, hbm],
        out_specs=(vmem, vmem, hbm, hbm),
        scratch_shapes=[
            pltpu.VMEM((width, hidden), half_type),
            pltpu.VMEM((hidden, width), half_type),
            pltpu.VMEM((total, tok_dev), half_type),
            pltpu.VMEM((total, 2 * width + 128), half_type),
            pltpu.VMEM((2 * total, 2 * width + 128), half_type),
            pltpu.VMEM((2 * total, width), half_type),
            pltpu.VMEM((2 * total, hidden), half_type),
            pltpu.VMEM((2 * total, hidden), half_type),
            pltpu.VMEM((2, total, width + 128), jnp.float32),
            pltpu.VMEM((2, total // 2, width + 128), jnp.float32),
            pltpu.VMEM((total, width + 128), half_type),
            pltpu.VMEM((total, width + 128), half_type),
            pltpu.VMEM((width, hidden), half_type),
            pltpu.VMEM((hidden, width), half_type),
            dma((2,)),
            dma((experts,)),
            dma((experts,)),
            dma((experts,)),
            dma((experts,)),
            dma((2,)),
            dma((2,)),
            dma((experts,)),
            dma((experts,)),
            dma((width // 256,)),
            dma((hidden // 256,)),
        ],
        compiler_params=pltpu.CompilerParams(
            collective_id=0, has_side_effects=True, vmem_limit_bytes=48 * 1024 * 1024
        ),
        cost_estimate=pl.CostEstimate(
            flops=20 * total * width * hidden,
            bytes_accessed=8 * width * hidden,
            transcendentals=2 * total * hidden,
        ),
    )(tokens, grad_out, probs, choices, router, w_in, w_out)
    return (grad_tokens, grad_w_in, grad_w_out, grad_logits)


def body(tokens, grad_out, probs, choices, w_in, w_out, router):
    experts, capacity = choices.shape
    owners = experts * lax.axis_size("hidden")
    slots = 2 * capacity // owners
    fits = (
        lax.axis_size("hidden") == 2
        and experts % 2 == 0
        and slots % 16 == 0
        and w_in.shape[0] == 1
        and 2 * experts <= 128
        and w_in.shape[1] % 256 == 0
        and w_in.shape[2] % 512 == 0
    )
    chosen = fused_body if fits else general_body
    return chosen(tokens, grad_out, probs, choices, w_in, w_out, router)


def solution(mesh):
    in_specs = (
        P(("groups", "expert", "hidden"), None),
        P(("groups", "expert", "hidden"), None),
        P(("groups", "expert", "hidden"), None),
        P("groups", None),
        P("expert", None, "hidden"),
        P("expert", "hidden", None),
        P(),
    )
    out_specs = (
        P(("groups", "expert", "hidden"), None),
        P(("groups", "expert"), None, "hidden"),
        P(("groups", "expert"), "hidden", None),
        P(("groups", "expert", "hidden"), None),
    )
    return jax.shard_map(body, mesh=mesh, in_specs=in_specs, out_specs=out_specs, check_vma=False)
```

```python
import functools
import math

import jax
import jax.numpy as jnp
from jax import lax
from jax.experimental import pallas as pl
from jax.experimental.pallas import tpu as pltpu
from jax.sharding import PartitionSpec as P

gelu_scale = math.sqrt(2.0 / math.pi)
cubic_coef = 0.044715


def gelu_parts(inputs):
    tanh_value = jnp.tanh(gelu_scale * (inputs + cubic_coef * inputs * inputs * inputs))
    gelu_value = 0.5 * inputs * (1.0 + tanh_value)
    gelu_slope = 0.5 * (1.0 + tanh_value) + 0.5 * inputs * (
        1.0 - tanh_value * tanh_value
    ) * gelu_scale * (1.0 + 3.0 * cubic_coef * inputs * inputs)
    return (gelu_value, gelu_slope)


def expert_pass(token_rows, grad_rows, gate_rows, w_first, w_second):
    leading = token_rows.shape[:-1]
    width = token_rows.shape[-1]
    flat_tokens = token_rows.reshape(-1, width)
    flat_grads = grad_rows.reshape(-1, width)
    flat_gates = gate_rows.reshape(-1)
    pre_act = jnp.dot(flat_tokens, w_first, preferred_element_type=jnp.float32)
    gelu_value, gelu_slope = gelu_parts(pre_act)
    activation = gelu_value.astype(jnp.bfloat16)
    branch_out = jnp.dot(activation, w_second, preferred_element_type=jnp.float32)
    gate_grad = jnp.sum(flat_grads.astype(jnp.float32) * branch_out, axis=-1)
    scaled_grad = (flat_gates.astype(jnp.float32)[:, None] * flat_grads.astype(jnp.float32)).astype(
        jnp.bfloat16
    )
    act_grad = lax.dot_general(
        scaled_grad, w_second, (((1,), (1,)), ((), ())), preferred_element_type=jnp.float32
    )
    pre_grad = (act_grad * gelu_slope).astype(jnp.bfloat16)
    input_part = lax.dot_general(
        pre_grad, w_first, (((1,), (1,)), ((), ())), preferred_element_type=jnp.float32
    )
    hidden_width = w_first.shape[1]
    return (
        input_part.reshape(leading + (width,)),
        gate_grad.reshape(leading),
        token_rows,
        activation.reshape(leading + (hidden_width,)),
        scaled_grad.reshape(leading + (width,)),
        pre_grad.reshape(leading + (hidden_width,)),
    )


def general_body(tokens, grad_out, probs, choices, w_in, w_out, router):
    tok_dev, width = tokens.shape
    experts, capacity = choices.shape
    expert_count = lax.axis_size("expert")
    hidden_count = lax.axis_size("hidden")
    owner_count = expert_count * hidden_count
    slot_count = 2 * capacity // owner_count
    slot_total = experts * slot_count
    my_owner = lax.axis_index("expert") * hidden_count + lax.axis_index("hidden")
    w_first = w_in[0]
    w_second = w_out[0]
    owners_of = choices // tok_dev
    before = jnp.sum((owners_of < my_owner).astype(jnp.int32), axis=1)
    mine_count = jnp.sum((owners_of == my_owner).astype(jnp.int32), axis=1)
    slot_rank = lax.broadcasted_iota(jnp.int32, (experts, slot_count), 1)
    position = before[:, None] + slot_rank
    pick_mask = (
        lax.broadcasted_iota(jnp.int32, (experts, slot_count, capacity), 2) == position[:, :, None]
    )
    picked = jnp.sum(jnp.where(pick_mask, choices[:, None, :], 0), axis=2)
    slot_token = jnp.where(
        slot_rank < mine_count[:, None], picked - my_owner * tok_dev, tok_dev
    ).reshape(-1)
    slot_expert = lax.broadcasted_iota(jnp.int32, (experts, slot_count), 0).reshape(-1)
    selector = slot_token[:, None] == lax.broadcasted_iota(jnp.int32, (slot_total, tok_dev), 1)
    select_half = selector.astype(jnp.bfloat16)
    select_full = selector.astype(jnp.float32)
    expert_mask = slot_expert[:, None] == lax.broadcasted_iota(jnp.int32, (slot_total, experts), 1)
    stacked = jnp.concatenate([tokens, grad_out], axis=1)
    picked_rows = jnp.dot(select_half, stacked, preferred_element_type=jnp.float32).astype(
        jnp.bfloat16
    )
    send_tokens = picked_rows[:, :width].reshape(experts, slot_count, width)
    send_grads = picked_rows[:, width:].reshape(experts, slot_count, width)
    prob_rows = jnp.dot(
        select_full, probs, precision=lax.Precision.HIGHEST, preferred_element_type=jnp.float32
    )
    send_gates = (
        jnp.sum(jnp.where(expert_mask, prob_rows, 0.0), axis=1)
        .astype(jnp.bfloat16)
        .reshape(experts, slot_count)
    )

    def doubled(array):
        spread = jnp.broadcast_to(array[:, None], (experts, hidden_count) + array.shape[1:])
        return spread.reshape((experts * hidden_count,) + array.shape[1:])

    results = expert_pass(
        lax.all_to_all(
            doubled(send_tokens), ("expert", "hidden"), split_axis=0, concat_axis=0, tiled=True
        ),
        lax.all_to_all(
            doubled(send_grads), ("expert", "hidden"), split_axis=0, concat_axis=0, tiled=True
        ),
        lax.all_to_all(
            doubled(send_gates), ("expert", "hidden"), split_axis=0, concat_axis=0, tiled=True
        ),
        w_first,
        w_second,
    )
    input_part, gate_part, token_rows, activation, scaled_grad, pre_grad = results
    hidden_width = w_first.shape[1]
    grad_first = lax.dot_general(
        token_rows.reshape(-1, width),
        pre_grad.reshape(-1, hidden_width),
        (((0,), (0,)), ((), ())),
        preferred_element_type=jnp.float32,
    )
    grad_second = lax.dot_general(
        activation.reshape(-1, hidden_width),
        scaled_grad.reshape(-1, width),
        (((0,), (0,)), ((), ())),
        preferred_element_type=jnp.float32,
    )
    grad_w_in = grad_first.astype(jnp.bfloat16)[None]
    grad_w_out = grad_second.astype(jnp.bfloat16)[None]
    back_rows, back_gates = (
        lax.all_to_all(input_part, ("expert", "hidden"), split_axis=0, concat_axis=0, tiled=True),
        lax.all_to_all(gate_part, ("expert", "hidden"), split_axis=0, concat_axis=0, tiled=True),
    )
    rows_back = jnp.sum(back_rows.reshape(experts, hidden_count, slot_count, width), axis=1)
    gates_back = jnp.sum(back_gates.reshape(experts, hidden_count, slot_count), axis=1)
    moe_grad = lax.dot_general(
        select_full,
        rows_back.reshape(slot_total, width),
        (((0,), (0,)), ((), ())),
        precision=lax.Precision.HIGHEST,
        preferred_element_type=jnp.float32,
    )
    gate_table = jnp.where(expert_mask, gates_back.reshape(-1)[:, None], 0.0)
    score_grad = lax.dot_general(
        select_full,
        gate_table,
        (((0,), (0,)), ((), ())),
        precision=lax.Precision.HIGHEST,
        preferred_element_type=jnp.float32,
    )
    grad_logits = probs * (score_grad - jnp.sum(probs * score_grad, axis=-1, keepdims=True))
    router_part = lax.dot_general(
        grad_logits,
        router,
        (((1,), (1,)), ((), ())),
        precision=lax.Precision.HIGHEST,
        preferred_element_type=jnp.float32,
    )
    grad_tokens = (moe_grad + router_part).astype(jnp.bfloat16)
    return (grad_tokens, grad_w_in, grad_w_out, grad_logits)


MESH = pl.DeviceIdType.MESH


def matmul(a, b, contract):
    return lax.dot_general(a, b, (contract, ((), ())), preferred_element_type=jnp.float32)


NN = ((1,), (0,))
NT = ((1,), (1,))
TN = ((0,), (0,))


def fused_kernel(
    experts,
    slots,
    tile,
    tokens_hbm,
    grads_hbm,
    probs_hbm,
    choices_hbm,
    router_hbm,
    w_in_hbm,
    w_out_hbm,
    grad_tokens_ref,
    grad_logits_ref,
    first_ref,
    second_ref,
    tokens_ref,
    grads_ref,
    probs_ref,
    choices_ref,
    router_ref,
    w_in_ref,
    w_out_ref,
    select_ref,
    send_ref,
    rows_ref,
    scaled_ref,
    act_ref,
    pre_grad_ref,
    part_ref,
    pair_ref,
    ret_ref,
    back_ref,
    load_sem,
    go_send,
    go_recv,
    fwd_send,
    fwd_recv,
    pair_send,
    pair_recv,
    ret_send,
    ret_recv,
):
    tok_dev, width = tokens_ref.shape
    hidden = w_in_ref.shape[1]
    half = experts // 2
    chunk = half * slots
    me = lax.axis_index("expert")
    core = lax.axis_index("hidden")
    base = (me * 2 + core) * tok_dev
    side = me // half
    place = me % half

    def target(step):
        where = side if step < half else 1 - side
        return where * half + (place + step) % half

    def source(step):
        where = side if step < half else 1 - side
        return where * half + (place + 2 * half - step) % half

    def direct_row(step):
        return (step // half) * 2 * chunk + (step % half) * slots

    sibling = {"hidden": 1 - core}
    barrier = pltpu.get_barrier_semaphore()
    for step in range(1, experts):
        pl.semaphore_signal(
            barrier, inc=1, device_id={"expert": target(step)}, device_id_type=MESH
        )
    pl.semaphore_signal(barrier, inc=1, device_id=sibling, device_id_type=MESH)
    loads = [
        pltpu.make_async_copy(taken, kept, load_sem.at[index])
        for index, (taken, kept) in enumerate(
            (
                (choices_hbm, choices_ref),
                (tokens_hbm, tokens_ref),
                (grads_hbm, grads_ref),
                (probs_hbm, probs_ref),
                (router_hbm, router_ref),
                (w_in_hbm.at[0], w_in_ref),
                (w_out_hbm.at[0], w_out_ref),
            )
        )
    ]
    for load in loads:
        load.start()

    def go_copy(step):
        return pltpu.make_async_remote_copy(
            src_ref=send_ref.at[pl.ds(step * slots, slots)],
            dst_ref=rows_ref.at[pl.ds(direct_row(step), slots)],
            send_sem=go_send.at[step],
            recv_sem=go_recv.at[step],
            device_id={"expert": target(step)},
            device_id_type=MESH,
        )

    def fwd_copy(step):
        return pltpu.make_async_remote_copy(
            src_ref=rows_ref.at[pl.ds(direct_row(step), slots)],
            dst_ref=rows_ref.at[pl.ds(direct_row(step) + chunk, slots)],
            send_sem=fwd_send.at[step],
            recv_sem=fwd_recv.at[step],
            device_id=sibling,
            device_id_type=MESH,
        )

    def pair_copy(part):
        return pltpu.make_async_remote_copy(
            src_ref=part_ref.at[part, pl.ds(chunk, chunk)],
            dst_ref=pair_ref.at[part],
            send_sem=pair_send.at[part],
            recv_sem=pair_recv.at[part],
            device_id=sibling,
            device_id_type=MESH,
        )

    def ret_copy(step):
        return pltpu.make_async_remote_copy(
            src_ref=ret_ref.at[pl.ds(step * slots, slots)],
            dst_ref=back_ref.at[pl.ds(step * slots, slots)],
            send_sem=ret_send.at[step],
            recv_sem=ret_recv.at[step],
            device_id={"expert": source(step)},
            device_id_type=MESH,
        )

    for load in loads[:4]:
        load.wait()
    probs = probs_ref[...]
    probs_half = probs.astype(jnp.bfloat16)
    capacity = choices_ref.shape[1]
    rank_gap = lax.broadcasted_iota(jnp.int32, (slots, capacity), 1) - lax.broadcasted_iota(
        jnp.int32, (slots, capacity), 0
    )
    rank_gap = rank_gap.astype(jnp.float32)
    token_id = lax.broadcasted_iota(jnp.int32, (tok_dev, capacity), 0) + base
    column = lax.broadcasted_iota(jnp.int32, (slots, experts), 1)

    def select(part):
        for step in range(part * half, (part + 1) * half):
            row = choices_ref[pl.ds(target(step), 1), :]
            before = jnp.sum(jnp.where(row < base, 1.0, 0.0), axis=1, keepdims=True)
            pick = jnp.where(rank_gap == before, 1.0, 0.0).astype(jnp.bfloat16)
            equal = jnp.where(token_id == row, 1.0, 0.0).astype(jnp.bfloat16)
            select_ref[pl.ds(step * slots, slots), :] = matmul(pick, equal, NT).astype(jnp.bfloat16)
        chosen = select_ref[pl.ds(part * chunk, chunk), :]
        token_rows = matmul(chosen, tokens_ref[...], NN).astype(jnp.bfloat16)
        grad_rows = matmul(chosen, grads_ref[...], NN).astype(jnp.bfloat16)
        gates = matmul(chosen, probs_half, NT)
        for index in range(half):
            step = part * half + index
            mine = slice(index * slots, (index + 1) * slots)
            gate = jnp.sum(
                jnp.where(column == target(step), gates[mine], 0.0), axis=1, keepdims=True
            )
            gate = jnp.broadcast_to(gate, (slots, 128)).astype(jnp.bfloat16)
            ref = rows_ref if step == 0 else send_ref
            at = pl.ds(step * slots, slots)
            ref[at, :width] = token_rows[mine]
            ref[at, width : 2 * width] = grad_rows[mine]
            ref[at, 2 * width :] = gate

    select(1)
    pl.semaphore_wait(barrier, experts)
    for step in range(half, experts):
        go_copy(step).start()
    select(0)
    for step in range(1, half):
        go_copy(step).start()

    def forward(part):
        for step in range(part * half, (part + 1) * half):
            if step:
                go_copy(step).wait_recv()
            fwd_copy(step).start()

    def compute(part):
        for step in range(part * half, (part + 1) * half):
            fwd_copy(step).wait_recv()
        rows = pl.ds(part * 2 * chunk, 2 * chunk)
        gate = rows_ref[rows, 2 * width :].astype(jnp.float32)
        wide_gate = jnp.concatenate([gate] * (width // 128), axis=1)
        scaled_ref[rows, :] = (
            wide_gate * rows_ref[rows, width : 2 * width].astype(jnp.float32)
        ).astype(jnp.bfloat16)
        part_ref[part] = jnp.zeros(part_ref.shape[1:], jnp.float32)

        def step_tile(index, carry):
            at = pl.ds(pl.multiple_of(index * tile, tile), tile)
            w_first = w_in_ref[:, at]
            w_second = w_out_ref[at, :]
            pre_act = matmul(rows_ref[rows, :width], w_first, NN)
            raw_grad = matmul(rows_ref[rows, width : 2 * width], w_second, NT)
            gelu_value, gelu_slope = gelu_parts(pre_act)
            act = gelu_value.astype(jnp.bfloat16)
            act_ref[rows, at] = act
            product = act.astype(jnp.float32) * raw_grad
            gate_tile = jnp.concatenate([gate] * (tile // 128), axis=1)
            pre_grad = (gate_tile * raw_grad * gelu_slope).astype(jnp.bfloat16)
            pre_grad_ref[rows, at] = pre_grad
            part_ref[part, :, :width] += matmul(pre_grad, w_first, NT)
            total = product[:, :128]
            for lane in range(128, tile, 128):
                total = total + product[:, lane : lane + 128]
            part_ref[part, :, width:] += total
            return carry

        lax.fori_loop(0, hidden // tile, step_tile, 0)
        pair_copy(part).start()

    lane = lax.broadcasted_iota(jnp.int32, (chunk, 128), 1)

    def give_back(part):
        pair_copy(part).wait_recv()
        total = part_ref[part, :chunk, :] + pair_ref[part]
        gate_grad = jnp.sum(total[:, width:], axis=1, keepdims=True)
        high = gate_grad.astype(jnp.bfloat16).astype(jnp.float32)
        low = gate_grad - high
        coded = jnp.where(lane == me, high, jnp.where(lane == me + experts, low, 0.0))
        values = total[:, :width].astype(jnp.bfloat16)
        coded = coded.astype(jnp.bfloat16)
        for index in range(half):
            step = part * half + index
            mine = slice(index * slots, (index + 1) * slots)
            ref = ret_ref if step else back_ref
            ref[pl.ds(step * slots, slots), :width] = values[mine]
            ref[pl.ds(step * slots, slots), width:] = coded[mine]
            if step:
                ret_copy(step).start()

    first_rows = 256
    second_rows = 256

    def first_grad(index, carry):
        at = pl.ds(pl.multiple_of(index * first_rows, first_rows), first_rows)
        first_ref[0, at, :] = matmul(rows_ref[:, at], pre_grad_ref[...], TN).astype(jnp.bfloat16)
        return carry

    def second_grad(index, carry):
        at = pl.ds(pl.multiple_of(index * second_rows, second_rows), second_rows)
        second_ref[0, at, :] = matmul(act_ref[:, at], scaled_ref[...], TN).astype(jnp.bfloat16)
        return carry

    forward(0)
    for load in loads[4:]:
        load.wait()
    compute(0)
    forward(1)
    give_back(0)
    compute(1)
    first_count = width // first_rows
    second_count = hidden // second_rows
    lax.fori_loop(0, 1, first_grad, 0)
    give_back(1)
    lax.fori_loop(1, first_count, first_grad, 0)
    lax.fori_loop(0, second_count, second_grad, 0)

    for step in range(1, experts):
        ret_copy(step).wait_recv()
    scores = matmul(back_ref[:, width:], select_ref[...], TN)
    score_grad = scores[:experts] + scores[experts : 2 * experts]
    grad_logits = probs * (score_grad - jnp.sum(probs * score_grad, axis=0, keepdims=True))
    grad_logits_ref[...] = grad_logits
    router_part = lax.dot_general(
        grad_logits,
        router_ref[...],
        (TN, ((), ())),
        precision=lax.Precision.HIGHEST,
        preferred_element_type=jnp.float32,
    )
    moe_grad = matmul(select_ref[...], back_ref[:, :width], TN)
    grad_tokens_ref[...] = (moe_grad + router_part).astype(jnp.bfloat16)

    for step in range(1, experts):
        go_copy(step).wait_send()
        ret_copy(step).wait_send()
    for step in range(experts):
        fwd_copy(step).wait_send()
    for part in range(2):
        pair_copy(part).wait_send()


def write_kernel(*refs):
    count = len(refs) // 2
    copies = [
        pltpu.make_async_copy(refs[index], refs[count + index], refs[-1].at[index])
        for index in range(count)
    ]
    for copy in copies:
        copy.start()
    for copy in copies:
        copy.wait()


def fused_body(tokens, grad_out, probs, choices, w_in, w_out, router):
    tok_dev, width = tokens.shape
    experts, capacity = choices.shape
    hidden = w_in.shape[2]
    slots = 2 * capacity // (experts * lax.axis_size("hidden"))
    total = experts * slots
    half_type = jnp.bfloat16
    vmem = pl.BlockSpec(memory_space=pltpu.VMEM)
    hbm = pl.BlockSpec(memory_space=pltpu.HBM)
    dma = pltpu.SemaphoreType.DMA
    shapes = (
        jax.ShapeDtypeStruct(tokens.shape, half_type),
        jax.ShapeDtypeStruct(probs.shape[::-1], jnp.float32),
        jax.ShapeDtypeStruct(w_in.shape, half_type),
        jax.ShapeDtypeStruct(w_out.shape, half_type),
    )
    held = pl.pallas_call(
        functools.partial(fused_kernel, experts, slots, 512),
        out_shape=shapes,
        in_specs=[hbm] * 7,
        out_specs=(vmem,) * 4,
        scratch_shapes=[
            pltpu.VMEM(tokens.shape, half_type),
            pltpu.VMEM(tokens.shape, half_type),
            pltpu.VMEM(probs.shape[::-1], jnp.float32),
            pltpu.VMEM(choices.shape, jnp.int32),
            pltpu.VMEM(router.shape[::-1], jnp.float32),
            pltpu.VMEM((width, hidden), half_type),
            pltpu.VMEM((hidden, width), half_type),
            pltpu.VMEM((total, tok_dev), half_type),
            pltpu.VMEM((total, 2 * width + 128), half_type),
            pltpu.VMEM((2 * total, 2 * width + 128), half_type),
            pltpu.VMEM((2 * total, width), half_type),
            pltpu.VMEM((2 * total, hidden), half_type),
            pltpu.VMEM((2 * total, hidden), half_type),
            pltpu.VMEM((2, total, width + 128), jnp.float32),
            pltpu.VMEM((2, total // 2, width + 128), jnp.float32),
            pltpu.VMEM((total, width + 128), half_type),
            pltpu.VMEM((total, width + 128), half_type),
            dma((7,)),
            dma((experts,)),
            dma((experts,)),
            dma((experts,)),
            dma((experts,)),
            dma((2,)),
            dma((2,)),
            dma((experts,)),
            dma((experts,)),
        ],
        compiler_params=pltpu.CompilerParams(
            collective_id=0, has_side_effects=True, vmem_limit_bytes=48 * 1024 * 1024
        ),
        cost_estimate=pl.CostEstimate(
            flops=20 * total * width * hidden,
            bytes_accessed=8 * width * hidden,
            transcendentals=2 * total * hidden,
        ),
    )(tokens, grad_out, probs.T, choices, router.T, w_in, w_out)
    grad_tokens, grad_logits, grad_w_in, grad_w_out = pl.pallas_call(
        write_kernel,
        out_shape=shapes,
        in_specs=[pl.BlockSpec(memory_space=pl.ANY)] * 4,
        out_specs=(hbm,) * 4,
        scratch_shapes=[dma((4,))],
        compiler_params=pltpu.CompilerParams(vmem_limit_bytes=1024 * 1024),
    )(*held)
    return (grad_tokens, grad_w_in, grad_w_out, grad_logits.T)


def body(tokens, grad_out, probs, choices, w_in, w_out, router):
    experts, capacity = choices.shape
    owners = experts * lax.axis_size("hidden")
    slots = 2 * capacity // owners
    fits = (
        lax.axis_size("hidden") == 2
        and experts % 2 == 0
        and slots % 16 == 0
        and w_in.shape[0] == 1
        and 2 * experts <= 128
        and w_in.shape[1] % 256 == 0
        and w_in.shape[2] % 512 == 0
    )
    chosen = fused_body if fits else general_body
    return chosen(tokens, grad_out, probs, choices, w_in, w_out, router)


def solution(mesh):
    in_specs = (
        P(("groups", "expert", "hidden"), None),
        P(("groups", "expert", "hidden"), None),
        P(("groups", "expert", "hidden"), None),
        P("groups", None),
        P("expert", None, "hidden"),
        P("expert", "hidden", None),
        P(),
    )
    out_specs = (
        P(("groups", "expert", "hidden"), None),
        P(("groups", "expert"), None, "hidden"),
        P(("groups", "expert"), "hidden", None),
        P(("groups", "expert", "hidden"), None),
    )
    return jax.shard_map(body, mesh=mesh, in_specs=in_specs, out_specs=out_specs, check_vma=False)
```

```python
import functools
import math

import jax
import jax.numpy as jnp
from jax import lax
from jax.experimental import pallas as pl
from jax.experimental.pallas import tpu as pltpu
from jax.sharding import PartitionSpec as P

gelu_scale = math.sqrt(2.0 / math.pi)
cubic_coef = 0.044715


def gelu_parts(inputs):
    tanh_value = jnp.tanh(gelu_scale * (inputs + cubic_coef * inputs * inputs * inputs))
    gelu_value = 0.5 * inputs * (1.0 + tanh_value)
    gelu_slope = 0.5 * (1.0 + tanh_value) + 0.5 * inputs * (
        1.0 - tanh_value * tanh_value
    ) * gelu_scale * (1.0 + 3.0 * cubic_coef * inputs * inputs)
    return (gelu_value, gelu_slope)


def expert_pass(token_rows, grad_rows, gate_rows, w_first, w_second):
    leading = token_rows.shape[:-1]
    width = token_rows.shape[-1]
    flat_tokens = token_rows.reshape(-1, width)
    flat_grads = grad_rows.reshape(-1, width)
    flat_gates = gate_rows.reshape(-1)
    pre_act = jnp.dot(flat_tokens, w_first, preferred_element_type=jnp.float32)
    gelu_value, gelu_slope = gelu_parts(pre_act)
    activation = gelu_value.astype(jnp.bfloat16)
    branch_out = jnp.dot(activation, w_second, preferred_element_type=jnp.float32)
    gate_grad = jnp.sum(flat_grads.astype(jnp.float32) * branch_out, axis=-1)
    scaled_grad = (flat_gates.astype(jnp.float32)[:, None] * flat_grads.astype(jnp.float32)).astype(
        jnp.bfloat16
    )
    act_grad = lax.dot_general(
        scaled_grad, w_second, (((1,), (1,)), ((), ())), preferred_element_type=jnp.float32
    )
    pre_grad = (act_grad * gelu_slope).astype(jnp.bfloat16)
    input_part = lax.dot_general(
        pre_grad, w_first, (((1,), (1,)), ((), ())), preferred_element_type=jnp.float32
    )
    hidden_width = w_first.shape[1]
    return (
        input_part.reshape(leading + (width,)),
        gate_grad.reshape(leading),
        token_rows,
        activation.reshape(leading + (hidden_width,)),
        scaled_grad.reshape(leading + (width,)),
        pre_grad.reshape(leading + (hidden_width,)),
    )


def general_body(tokens, grad_out, probs, choices, w_in, w_out, router):
    tok_dev, width = tokens.shape
    experts, capacity = choices.shape
    expert_count = lax.axis_size("expert")
    hidden_count = lax.axis_size("hidden")
    owner_count = expert_count * hidden_count
    slot_count = 2 * capacity // owner_count
    slot_total = experts * slot_count
    my_owner = lax.axis_index("expert") * hidden_count + lax.axis_index("hidden")
    w_first = w_in[0]
    w_second = w_out[0]
    owners_of = choices // tok_dev
    before = jnp.sum((owners_of < my_owner).astype(jnp.int32), axis=1)
    mine_count = jnp.sum((owners_of == my_owner).astype(jnp.int32), axis=1)
    slot_rank = lax.broadcasted_iota(jnp.int32, (experts, slot_count), 1)
    position = before[:, None] + slot_rank
    pick_mask = (
        lax.broadcasted_iota(jnp.int32, (experts, slot_count, capacity), 2) == position[:, :, None]
    )
    picked = jnp.sum(jnp.where(pick_mask, choices[:, None, :], 0), axis=2)
    slot_token = jnp.where(
        slot_rank < mine_count[:, None], picked - my_owner * tok_dev, tok_dev
    ).reshape(-1)
    slot_expert = lax.broadcasted_iota(jnp.int32, (experts, slot_count), 0).reshape(-1)
    selector = slot_token[:, None] == lax.broadcasted_iota(jnp.int32, (slot_total, tok_dev), 1)
    select_half = selector.astype(jnp.bfloat16)
    select_full = selector.astype(jnp.float32)
    expert_mask = slot_expert[:, None] == lax.broadcasted_iota(jnp.int32, (slot_total, experts), 1)
    stacked = jnp.concatenate([tokens, grad_out], axis=1)
    picked_rows = jnp.dot(select_half, stacked, preferred_element_type=jnp.float32).astype(
        jnp.bfloat16
    )
    send_tokens = picked_rows[:, :width].reshape(experts, slot_count, width)
    send_grads = picked_rows[:, width:].reshape(experts, slot_count, width)
    prob_rows = jnp.dot(
        select_full, probs, precision=lax.Precision.HIGHEST, preferred_element_type=jnp.float32
    )
    send_gates = (
        jnp.sum(jnp.where(expert_mask, prob_rows, 0.0), axis=1)
        .astype(jnp.bfloat16)
        .reshape(experts, slot_count)
    )

    def doubled(array):
        spread = jnp.broadcast_to(array[:, None], (experts, hidden_count) + array.shape[1:])
        return spread.reshape((experts * hidden_count,) + array.shape[1:])

    results = expert_pass(
        lax.all_to_all(
            doubled(send_tokens), ("expert", "hidden"), split_axis=0, concat_axis=0, tiled=True
        ),
        lax.all_to_all(
            doubled(send_grads), ("expert", "hidden"), split_axis=0, concat_axis=0, tiled=True
        ),
        lax.all_to_all(
            doubled(send_gates), ("expert", "hidden"), split_axis=0, concat_axis=0, tiled=True
        ),
        w_first,
        w_second,
    )
    input_part, gate_part, token_rows, activation, scaled_grad, pre_grad = results
    hidden_width = w_first.shape[1]
    grad_first = lax.dot_general(
        token_rows.reshape(-1, width),
        pre_grad.reshape(-1, hidden_width),
        (((0,), (0,)), ((), ())),
        preferred_element_type=jnp.float32,
    )
    grad_second = lax.dot_general(
        activation.reshape(-1, hidden_width),
        scaled_grad.reshape(-1, width),
        (((0,), (0,)), ((), ())),
        preferred_element_type=jnp.float32,
    )
    grad_w_in = grad_first.astype(jnp.bfloat16)[None]
    grad_w_out = grad_second.astype(jnp.bfloat16)[None]
    back_rows, back_gates = (
        lax.all_to_all(input_part, ("expert", "hidden"), split_axis=0, concat_axis=0, tiled=True),
        lax.all_to_all(gate_part, ("expert", "hidden"), split_axis=0, concat_axis=0, tiled=True),
    )
    rows_back = jnp.sum(back_rows.reshape(experts, hidden_count, slot_count, width), axis=1)
    gates_back = jnp.sum(back_gates.reshape(experts, hidden_count, slot_count), axis=1)
    moe_grad = lax.dot_general(
        select_full,
        rows_back.reshape(slot_total, width),
        (((0,), (0,)), ((), ())),
        precision=lax.Precision.HIGHEST,
        preferred_element_type=jnp.float32,
    )
    gate_table = jnp.where(expert_mask, gates_back.reshape(-1)[:, None], 0.0)
    score_grad = lax.dot_general(
        select_full,
        gate_table,
        (((0,), (0,)), ((), ())),
        precision=lax.Precision.HIGHEST,
        preferred_element_type=jnp.float32,
    )
    grad_logits = probs * (score_grad - jnp.sum(probs * score_grad, axis=-1, keepdims=True))
    router_part = lax.dot_general(
        grad_logits,
        router,
        (((1,), (1,)), ((), ())),
        precision=lax.Precision.HIGHEST,
        preferred_element_type=jnp.float32,
    )
    grad_tokens = (moe_grad + router_part).astype(jnp.bfloat16)
    return (grad_tokens, grad_w_in, grad_w_out, grad_logits)


MESH = pl.DeviceIdType.MESH


def matmul(a, b, contract):
    return lax.dot_general(a, b, (contract, ((), ())), preferred_element_type=jnp.float32)


NN = ((1,), (0,))
NT = ((1,), (1,))
TN = ((0,), (0,))


def fused_kernel(
    experts,
    slots,
    tile,
    tokens_ref,
    table_ref,
    w_in_hbm,
    w_out_hbm,
    grad_tokens_ref,
    grad_logits_ref,
    first_ref,
    second_ref,
    w_in_ref,
    w_out_ref,
    select_ref,
    send_ref,
    rows_ref,
    scaled_ref,
    act_ref,
    pre_grad_ref,
    part_ref,
    pair_ref,
    ret_ref,
    back_ref,
    load_sem,
    go_send,
    go_recv,
    fwd_send,
    fwd_recv,
    pair_send,
    pair_recv,
    ret_send,
    ret_recv,
):
    tok_dev = tokens_ref.shape[0]
    width = w_in_ref.shape[0]
    capacity = table_ref.shape[1] - tok_dev - width
    hidden = w_in_ref.shape[1]
    half = experts // 2
    chunk = half * slots
    me = lax.axis_index("expert")
    core = lax.axis_index("hidden")
    base = (me * 2 + core) * tok_dev
    side = me // half
    place = me % half

    def target(step):
        where = side if step < half else 1 - side
        return where * half + (place + step) % half

    def source(step):
        where = side if step < half else 1 - side
        return where * half + (place + 2 * half - step) % half

    parts = ((0, half), (half, half // 2), (half + half // 2, half - half // 2))

    def place_of(step):
        return [part for part in parts if part[0] <= step < sum(part)][0]

    def direct_row(step):
        start, count = place_of(step)
        return (step + start) * slots

    sibling = {"hidden": 1 - core}
    barrier = pltpu.get_barrier_semaphore()
    for step in range(1, experts):
        pl.semaphore_signal(
            barrier, inc=1, device_id={"expert": target(step)}, device_id_type=MESH
        )
    pl.semaphore_signal(barrier, inc=1, device_id=sibling, device_id_type=MESH)
    loads = [
        pltpu.make_async_copy(taken, kept, load_sem.at[index])
        for index, (taken, kept) in enumerate(
            (
                (w_in_hbm.at[0], w_in_ref),
                (w_out_hbm.at[0], w_out_ref),
            )
        )
    ]
    for load in loads:
        load.start()

    def go_copy(step):
        return pltpu.make_async_remote_copy(
            src_ref=send_ref.at[pl.ds(step * slots, slots)],
            dst_ref=rows_ref.at[pl.ds(direct_row(step), slots)],
            send_sem=go_send.at[step],
            recv_sem=go_recv.at[step],
            device_id={"expert": target(step)},
            device_id_type=MESH,
        )

    def fwd_copy(step):
        return pltpu.make_async_remote_copy(
            src_ref=rows_ref.at[pl.ds(direct_row(step), slots)],
            dst_ref=rows_ref.at[pl.ds(direct_row(step) + place_of(step)[1] * slots, slots)],
            send_sem=fwd_send.at[step],
            recv_sem=fwd_recv.at[step],
            device_id=sibling,
            device_id_type=MESH,
        )

    def pair_copy(part):
        start, count = parts[part]
        return pltpu.make_async_remote_copy(
            src_ref=part_ref.at[pl.ds((2 * start + count) * slots, count * slots)],
            dst_ref=pair_ref.at[pl.ds(start * slots, count * slots)],
            send_sem=pair_send.at[part],
            recv_sem=pair_recv.at[part],
            device_id=sibling,
            device_id_type=MESH,
        )

    def ret_copy(step):
        return pltpu.make_async_remote_copy(
            src_ref=ret_ref.at[pl.ds(step * slots, slots)],
            dst_ref=back_ref.at[pl.ds(step * slots, slots)],
            send_sem=ret_send.at[step],
            recv_sem=ret_recv.at[step],
            device_id={"expert": source(step)},
            device_id_type=MESH,
        )

    probs = table_ref[:, :tok_dev]
    probs_half = probs.astype(jnp.bfloat16)
    rank_gap = lax.broadcasted_iota(jnp.int32, (slots, capacity), 1) - lax.broadcasted_iota(
        jnp.int32, (slots, capacity), 0
    )
    rank_gap = rank_gap.astype(jnp.float32)
    token_id = lax.broadcasted_iota(jnp.int32, (tok_dev, capacity), 0) + base
    token_id = token_id.astype(jnp.float32)
    first_token = token_id[:1, :]
    column = lax.broadcasted_iota(jnp.int32, (slots, experts), 1)

    def select(part):
        for step in range(part * half, (part + 1) * half):
            row = table_ref[pl.ds(target(step), 1), tok_dev + width :]
            before = jnp.sum(jnp.where(row < first_token, 1.0, 0.0), axis=1, keepdims=True)
            pick = jnp.where(rank_gap == before, 1.0, 0.0).astype(jnp.bfloat16)
            equal = jnp.where(token_id == row, 1.0, 0.0).astype(jnp.bfloat16)
            select_ref[pl.ds(step * slots, slots), :] = matmul(pick, equal, NT).astype(jnp.bfloat16)
        chosen = select_ref[pl.ds(part * chunk, chunk), :]
        both_rows = matmul(chosen, tokens_ref[...], NN).astype(jnp.bfloat16)
        gates = matmul(chosen, probs_half, NT)
        for index in range(half):
            step = part * half + index
            mine = slice(index * slots, (index + 1) * slots)
            gate = jnp.sum(
                jnp.where(column == target(step), gates[mine], 0.0), axis=1, keepdims=True
            )
            gate = jnp.broadcast_to(gate, (slots, 128)).astype(jnp.bfloat16)
            ref = rows_ref if step == 0 else send_ref
            at = pl.ds(step * slots, slots)
            ref[at, : 2 * width] = both_rows[mine]
            ref[at, 2 * width :] = gate

    select(1)
    pl.semaphore_wait(barrier, experts)
    for step in range(half, sum(parts[1])):
        go_copy(step).start()
    select(0)
    for step in range(1, half):
        go_copy(step).start()
    for step in range(parts[2][0], experts):
        go_copy(step).start()

    def forward(part):
        for step in range(parts[part][0], sum(parts[part])):
            if step:
                go_copy(step).wait_recv()
            fwd_copy(step).start()

    def compute(part):
        start, count = parts[part]
        for step in range(start, start + count):
            fwd_copy(step).wait_recv()
        rows = pl.ds(2 * start * slots, 2 * count * slots)
        gate = rows_ref[rows, 2 * width :].astype(jnp.float32)
        wide_gate = jnp.concatenate([gate] * (width // 128), axis=1)
        scaled_ref[rows, :] = (
            wide_gate * rows_ref[rows, width : 2 * width].astype(jnp.float32)
        ).astype(jnp.bfloat16)
        part_ref[rows, :] = jnp.zeros((2 * count * slots, width + 128), jnp.float32)

        def step_tile(index, carry):
            at = pl.ds(pl.multiple_of(index * tile, tile), tile)
            w_first = w_in_ref[:, at]
            w_second = w_out_ref[at, :]
            pre_act = matmul(rows_ref[rows, :width], w_first, NN)
            raw_grad = matmul(rows_ref[rows, width : 2 * width], w_second, NT)
            gelu_value, gelu_slope = gelu_parts(pre_act)
            act = gelu_value.astype(jnp.bfloat16)
            act_ref[rows, at] = act
            product = act.astype(jnp.float32) * raw_grad
            gate_tile = jnp.concatenate([gate] * (tile // 128), axis=1)
            pre_grad = (gate_tile * raw_grad * gelu_slope).astype(jnp.bfloat16)
            pre_grad_ref[rows, at] = pre_grad
            part_ref[rows, :width] += matmul(pre_grad, w_first, NT)
            total = product[:, :128]
            for lane in range(128, tile, 128):
                total = total + product[:, lane : lane + 128]
            part_ref[rows, width:] += total
            return carry

        lax.fori_loop(0, hidden // tile, step_tile, 0)
        pair_copy(part).start()

    def give_back(part):
        pair_copy(part).wait_recv()
        start, count = parts[part]
        lane = lax.broadcasted_iota(jnp.int32, (count * slots, 128), 1)
        own = part_ref[pl.ds(2 * start * slots, count * slots), :]
        total = own + pair_ref[pl.ds(start * slots, count * slots), :]
        gate_grad = jnp.sum(total[:, width:], axis=1, keepdims=True)
        high = gate_grad.astype(jnp.bfloat16).astype(jnp.float32)
        low = gate_grad - high
        coded = jnp.where(lane == me, high, jnp.where(lane == me + experts, low, 0.0))
        values = total[:, :width].astype(jnp.bfloat16)
        coded = coded.astype(jnp.bfloat16)
        for index in range(count):
            step = start + index
            mine = slice(index * slots, (index + 1) * slots)
            ref = ret_ref if step else back_ref
            ref[pl.ds(step * slots, slots), :width] = values[mine]
            ref[pl.ds(step * slots, slots), width:] = coded[mine]
            if step:
                ret_copy(step).start()

    first_rows = 256
    second_rows = 256

    def first_grad(index, carry):
        at = pl.ds(pl.multiple_of(index * first_rows, first_rows), first_rows)
        first_ref[0, at, :] = matmul(rows_ref[:, at], pre_grad_ref[...], TN).astype(jnp.bfloat16)
        return carry

    def second_grad(index, carry):
        at = pl.ds(pl.multiple_of(index * second_rows, second_rows), second_rows)
        second_ref[0, at, :] = matmul(act_ref[:, at], scaled_ref[...], TN).astype(jnp.bfloat16)
        return carry

    first_count = width // first_rows
    second_count = hidden // second_rows
    forward(0)
    for load in loads:
        load.wait()
    compute(0)
    forward(1)
    give_back(0)
    compute(1)
    forward(2)
    give_back(1)
    compute(2)
    lax.fori_loop(0, 1, first_grad, 0)
    give_back(2)
    lax.fori_loop(1, first_count, first_grad, 0)
    lax.fori_loop(0, second_count, second_grad, 0)

    def collect(start, stop):
        for step in range(max(start, 1), stop):
            ret_copy(step).wait_recv()
        rows = pl.ds(start * slots, (stop - start) * slots)
        scores = matmul(back_ref[rows, width:], select_ref[rows, :], TN)
        return matmul(select_ref[rows, :], back_ref[rows, :width], TN), scores

    early_grad, early_scores = collect(0, half)
    late_grad, late_scores = collect(half, experts)
    scores = early_scores + late_scores
    score_grad = scores[:experts] + scores[experts : 2 * experts]
    grad_logits = probs * (score_grad - jnp.sum(probs * score_grad, axis=0, keepdims=True))
    grad_logits_ref[...] = grad_logits
    router_part = lax.dot_general(
        grad_logits,
        table_ref[:, tok_dev : tok_dev + width],
        (TN, ((), ())),
        precision=lax.Precision.HIGHEST,
        preferred_element_type=jnp.float32,
    )
    grad_tokens_ref[...] = (early_grad + late_grad + router_part).astype(jnp.bfloat16)

    for step in range(1, experts):
        go_copy(step).wait_send()
        ret_copy(step).wait_send()
    for step in range(experts):
        fwd_copy(step).wait_send()
    for part in range(len(parts)):
        pair_copy(part).wait_send()


def write_kernel(*refs):
    count = len(refs) // 2
    copies = [
        pltpu.make_async_copy(refs[index], refs[count + index], refs[-1].at[index])
        for index in range(count)
    ]
    for copy in copies:
        copy.start()
    for copy in copies:
        copy.wait()


def fused_body(tokens, grad_out, probs, choices, w_in, w_out, router):
    tok_dev, width = tokens.shape
    experts, capacity = choices.shape
    hidden = w_in.shape[2]
    slots = 2 * capacity // (experts * lax.axis_size("hidden"))
    total = experts * slots
    half_type = jnp.bfloat16
    vmem = pl.BlockSpec(memory_space=pltpu.VMEM)
    hbm = pl.BlockSpec(memory_space=pltpu.HBM)
    dma = pltpu.SemaphoreType.DMA
    shapes = (
        jax.ShapeDtypeStruct(tokens.shape, half_type),
        jax.ShapeDtypeStruct(probs.shape[::-1], jnp.float32),
        jax.ShapeDtypeStruct(w_in.shape, half_type),
        jax.ShapeDtypeStruct(w_out.shape, half_type),
    )
    stacked = jnp.concatenate([tokens, grad_out], axis=1)
    table = jnp.concatenate([probs.T, router.T, choices.astype(jnp.float32)], axis=1)
    held = pl.pallas_call(
        functools.partial(fused_kernel, experts, slots, 512),
        out_shape=shapes,
        in_specs=[vmem, vmem, hbm, hbm],
        out_specs=(vmem,) * 4,
        scratch_shapes=[
            pltpu.VMEM((width, hidden), half_type),
            pltpu.VMEM((hidden, width), half_type),
            pltpu.VMEM((total, tok_dev), half_type),
            pltpu.VMEM((total, 2 * width + 128), half_type),
            pltpu.VMEM((2 * total, 2 * width + 128), half_type),
            pltpu.VMEM((2 * total, width), half_type),
            pltpu.VMEM((2 * total, hidden), half_type),
            pltpu.VMEM((2 * total, hidden), half_type),
            pltpu.VMEM((2 * total, width + 128), jnp.float32),
            pltpu.VMEM((total, width + 128), jnp.float32),
            pltpu.VMEM((total, width + 128), half_type),
            pltpu.VMEM((total, width + 128), half_type),
            dma((2,)),
            dma((experts,)),
            dma((experts,)),
            dma((experts,)),
            dma((experts,)),
            dma((3,)),
            dma((3,)),
            dma((experts,)),
            dma((experts,)),
        ],
        compiler_params=pltpu.CompilerParams(
            collective_id=0, has_side_effects=True, vmem_limit_bytes=48 * 1024 * 1024
        ),
        cost_estimate=pl.CostEstimate(
            flops=20 * total * width * hidden,
            bytes_accessed=8 * width * hidden,
            transcendentals=2 * total * hidden,
        ),
    )(stacked, table, w_in, w_out)
    grad_tokens, grad_logits, grad_w_in, grad_w_out = pl.pallas_call(
        write_kernel,
        out_shape=shapes,
        in_specs=[pl.BlockSpec(memory_space=pl.ANY)] * 4,
        out_specs=(hbm,) * 4,
        scratch_shapes=[dma((4,))],
        compiler_params=pltpu.CompilerParams(vmem_limit_bytes=1024 * 1024),
    )(*held)
    return (grad_tokens, grad_w_in, grad_w_out, grad_logits.T)


def body(tokens, grad_out, probs, choices, w_in, w_out, router):
    experts, capacity = choices.shape
    owners = experts * lax.axis_size("hidden")
    slots = 2 * capacity // owners
    fits = (
        lax.axis_size("hidden") == 2
        and experts % 4 == 0
        and slots % 16 == 0
        and tokens.shape[0] % 128 == 0
        and w_in.shape[0] == 1
        and 2 * experts <= 128
        and w_in.shape[1] % 256 == 0
        and w_in.shape[2] % 512 == 0
    )
    chosen = fused_body if fits else general_body
    return chosen(tokens, grad_out, probs, choices, w_in, w_out, router)


def solution(mesh):
    in_specs = (
        P(("groups", "expert", "hidden"), None),
        P(("groups", "expert", "hidden"), None),
        P(("groups", "expert", "hidden"), None),
        P("groups", None),
        P("expert", None, "hidden"),
        P("expert", "hidden", None),
        P(),
    )
    out_specs = (
        P(("groups", "expert", "hidden"), None),
        P(("groups", "expert"), None, "hidden"),
        P(("groups", "expert"), "hidden", None),
        P(("groups", "expert", "hidden"), None),
    )
    return jax.shard_map(body, mesh=mesh, in_specs=in_specs, out_specs=out_specs, check_vma=False)
```

```python
import functools
import math

import jax
import jax.numpy as jnp
from jax import lax
from jax.experimental import pallas as pl
from jax.experimental.pallas import tpu as pltpu
from jax.sharding import PartitionSpec as P

gelu_scale = math.sqrt(2.0 / math.pi)
cubic_coef = 0.044715


def gelu_parts(inputs):
    tanh_value = jnp.tanh(gelu_scale * (inputs + cubic_coef * inputs * inputs * inputs))
    gelu_value = 0.5 * inputs * (1.0 + tanh_value)
    gelu_slope = 0.5 * (1.0 + tanh_value) + 0.5 * inputs * (
        1.0 - tanh_value * tanh_value
    ) * gelu_scale * (1.0 + 3.0 * cubic_coef * inputs * inputs)
    return (gelu_value, gelu_slope)


def expert_pass(token_rows, grad_rows, gate_rows, w_first, w_second):
    leading = token_rows.shape[:-1]
    width = token_rows.shape[-1]
    flat_tokens = token_rows.reshape(-1, width)
    flat_grads = grad_rows.reshape(-1, width)
    flat_gates = gate_rows.reshape(-1)
    pre_act = jnp.dot(flat_tokens, w_first, preferred_element_type=jnp.float32)
    gelu_value, gelu_slope = gelu_parts(pre_act)
    activation = gelu_value.astype(jnp.bfloat16)
    branch_out = jnp.dot(activation, w_second, preferred_element_type=jnp.float32)
    gate_grad = jnp.sum(flat_grads.astype(jnp.float32) * branch_out, axis=-1)
    scaled_grad = (flat_gates.astype(jnp.float32)[:, None] * flat_grads.astype(jnp.float32)).astype(
        jnp.bfloat16
    )
    act_grad = lax.dot_general(
        scaled_grad, w_second, (((1,), (1,)), ((), ())), preferred_element_type=jnp.float32
    )
    pre_grad = (act_grad * gelu_slope).astype(jnp.bfloat16)
    input_part = lax.dot_general(
        pre_grad, w_first, (((1,), (1,)), ((), ())), preferred_element_type=jnp.float32
    )
    hidden_width = w_first.shape[1]
    return (
        input_part.reshape(leading + (width,)),
        gate_grad.reshape(leading),
        token_rows,
        activation.reshape(leading + (hidden_width,)),
        scaled_grad.reshape(leading + (width,)),
        pre_grad.reshape(leading + (hidden_width,)),
    )


def general_body(tokens, grad_out, probs, choices, w_in, w_out, router):
    tok_dev, width = tokens.shape
    experts, capacity = choices.shape
    expert_count = lax.axis_size("expert")
    hidden_count = lax.axis_size("hidden")
    owner_count = expert_count * hidden_count
    slot_count = 2 * capacity // owner_count
    slot_total = experts * slot_count
    my_owner = lax.axis_index("expert") * hidden_count + lax.axis_index("hidden")
    w_first = w_in[0]
    w_second = w_out[0]
    owners_of = choices // tok_dev
    before = jnp.sum((owners_of < my_owner).astype(jnp.int32), axis=1)
    mine_count = jnp.sum((owners_of == my_owner).astype(jnp.int32), axis=1)
    slot_rank = lax.broadcasted_iota(jnp.int32, (experts, slot_count), 1)
    position = before[:, None] + slot_rank
    pick_mask = (
        lax.broadcasted_iota(jnp.int32, (experts, slot_count, capacity), 2) == position[:, :, None]
    )
    picked = jnp.sum(jnp.where(pick_mask, choices[:, None, :], 0), axis=2)
    slot_token = jnp.where(
        slot_rank < mine_count[:, None], picked - my_owner * tok_dev, tok_dev
    ).reshape(-1)
    slot_expert = lax.broadcasted_iota(jnp.int32, (experts, slot_count), 0).reshape(-1)
    selector = slot_token[:, None] == lax.broadcasted_iota(jnp.int32, (slot_total, tok_dev), 1)
    select_half = selector.astype(jnp.bfloat16)
    select_full = selector.astype(jnp.float32)
    expert_mask = slot_expert[:, None] == lax.broadcasted_iota(jnp.int32, (slot_total, experts), 1)
    stacked = jnp.concatenate([tokens, grad_out], axis=1)
    picked_rows = jnp.dot(select_half, stacked, preferred_element_type=jnp.float32).astype(
        jnp.bfloat16
    )
    send_tokens = picked_rows[:, :width].reshape(experts, slot_count, width)
    send_grads = picked_rows[:, width:].reshape(experts, slot_count, width)
    prob_rows = jnp.dot(
        select_full, probs, precision=lax.Precision.HIGHEST, preferred_element_type=jnp.float32
    )
    send_gates = (
        jnp.sum(jnp.where(expert_mask, prob_rows, 0.0), axis=1)
        .astype(jnp.bfloat16)
        .reshape(experts, slot_count)
    )

    def doubled(array):
        spread = jnp.broadcast_to(array[:, None], (experts, hidden_count) + array.shape[1:])
        return spread.reshape((experts * hidden_count,) + array.shape[1:])

    results = expert_pass(
        lax.all_to_all(
            doubled(send_tokens), ("expert", "hidden"), split_axis=0, concat_axis=0, tiled=True
        ),
        lax.all_to_all(
            doubled(send_grads), ("expert", "hidden"), split_axis=0, concat_axis=0, tiled=True
        ),
        lax.all_to_all(
            doubled(send_gates), ("expert", "hidden"), split_axis=0, concat_axis=0, tiled=True
        ),
        w_first,
        w_second,
    )
    input_part, gate_part, token_rows, activation, scaled_grad, pre_grad = results
    hidden_width = w_first.shape[1]
    grad_first = lax.dot_general(
        token_rows.reshape(-1, width),
        pre_grad.reshape(-1, hidden_width),
        (((0,), (0,)), ((), ())),
        preferred_element_type=jnp.float32,
    )
    grad_second = lax.dot_general(
        activation.reshape(-1, hidden_width),
        scaled_grad.reshape(-1, width),
        (((0,), (0,)), ((), ())),
        preferred_element_type=jnp.float32,
    )
    grad_w_in = grad_first.astype(jnp.bfloat16)[None]
    grad_w_out = grad_second.astype(jnp.bfloat16)[None]
    back_rows, back_gates = (
        lax.all_to_all(input_part, ("expert", "hidden"), split_axis=0, concat_axis=0, tiled=True),
        lax.all_to_all(gate_part, ("expert", "hidden"), split_axis=0, concat_axis=0, tiled=True),
    )
    rows_back = jnp.sum(back_rows.reshape(experts, hidden_count, slot_count, width), axis=1)
    gates_back = jnp.sum(back_gates.reshape(experts, hidden_count, slot_count), axis=1)
    moe_grad = lax.dot_general(
        select_full,
        rows_back.reshape(slot_total, width),
        (((0,), (0,)), ((), ())),
        precision=lax.Precision.HIGHEST,
        preferred_element_type=jnp.float32,
    )
    gate_table = jnp.where(expert_mask, gates_back.reshape(-1)[:, None], 0.0)
    score_grad = lax.dot_general(
        select_full,
        gate_table,
        (((0,), (0,)), ((), ())),
        precision=lax.Precision.HIGHEST,
        preferred_element_type=jnp.float32,
    )
    grad_logits = probs * (score_grad - jnp.sum(probs * score_grad, axis=-1, keepdims=True))
    router_part = lax.dot_general(
        grad_logits,
        router,
        (((1,), (1,)), ((), ())),
        precision=lax.Precision.HIGHEST,
        preferred_element_type=jnp.float32,
    )
    grad_tokens = (moe_grad + router_part).astype(jnp.bfloat16)
    return (grad_tokens, grad_w_in, grad_w_out, grad_logits)


MESH = pl.DeviceIdType.MESH


def matmul(a, b, contract):
    return lax.dot_general(a, b, (contract, ((), ())), preferred_element_type=jnp.float32)


NN = ((1,), (0,))
NT = ((1,), (1,))
TN = ((0,), (0,))


def fused_kernel(
    experts,
    slots,
    tile,
    tokens_ref,
    table_ref,
    w_in_hbm,
    w_out_hbm,
    grad_tokens_ref,
    grad_logits_ref,
    first_ref,
    second_ref,
    w_in_ref,
    w_out_ref,
    w_in_t_ref,
    w_out_t_ref,
    select_ref,
    send_ref,
    rows_ref,
    scaled_ref,
    act_ref,
    pre_grad_ref,
    part_ref,
    pair_ref,
    ret_ref,
    back_ref,
    gate_out_ref,
    gate_in_ref,
    slope_out_ref,
    slope_in_ref,
    load_sem,
    go_send,
    go_recv,
    fwd_send,
    fwd_recv,
    pair_send,
    pair_recv,
    ret_send,
    ret_recv,
    gate_send,
    gate_recv,
    gate_fwd_send,
    gate_fwd_recv,
    slope_send,
    slope_recv,
):
    tok_dev = tokens_ref.shape[0]
    width = w_in_ref.shape[0]
    capacity = table_ref.shape[1] - tok_dev - width
    hidden = w_in_ref.shape[1]
    half = experts // 2
    chunk = half * slots
    me = lax.axis_index("expert")
    core = lax.axis_index("hidden")
    base = (me * 2 + core) * tok_dev
    side = me // half
    place = me % half

    def target(step):
        where = side if step < half else 1 - side
        return where * half + (place + step) % half

    def source(step):
        where = side if step < half else 1 - side
        return where * half + (place + 2 * half - step) % half

    parts = ((0, half), (half, half // 2), (half + half // 2, half - half // 2))

    def place_of(step):
        return [part for part in parts if part[0] <= step < sum(part)][0]

    def direct_row(step):
        start, count = place_of(step)
        return (step + start) * slots

    sibling = {"hidden": 1 - core}
    barrier = pltpu.get_barrier_semaphore()
    for step in range(1, experts):
        pl.semaphore_signal(
            barrier, inc=1, device_id={"expert": target(step)}, device_id_type=MESH
        )
    pl.semaphore_signal(barrier, inc=1, device_id=sibling, device_id_type=MESH)
    loads = [
        pltpu.make_async_copy(taken, kept, load_sem.at[index])
        for index, (taken, kept) in enumerate(
            (
                (w_in_hbm.at[0], w_in_ref),
                (w_out_hbm.at[0], w_out_ref),
            )
        )
    ]
    for load in loads:
        load.start()

    def go_copy(step):
        return pltpu.make_async_remote_copy(
            src_ref=send_ref.at[pl.ds(step * slots, slots)],
            dst_ref=rows_ref.at[pl.ds(direct_row(step), slots)],
            send_sem=go_send.at[step],
            recv_sem=go_recv.at[step],
            device_id={"expert": target(step)},
            device_id_type=MESH,
        )

    def fwd_copy(step):
        return pltpu.make_async_remote_copy(
            src_ref=rows_ref.at[pl.ds(direct_row(step), slots)],
            dst_ref=rows_ref.at[pl.ds(direct_row(step) + place_of(step)[1] * slots, slots)],
            send_sem=fwd_send.at[step],
            recv_sem=fwd_recv.at[step],
            device_id=sibling,
            device_id_type=MESH,
        )

    def gate_copy(step):
        return pltpu.make_async_remote_copy(
            src_ref=gate_out_ref.at[step],
            dst_ref=gate_in_ref.at[direct_row(step) // slots],
            send_sem=gate_send.at[step],
            recv_sem=gate_recv.at[step],
            device_id={"expert": target(step)},
            device_id_type=MESH,
        )

    def gate_fwd_copy(step):
        row = direct_row(step) // slots
        return pltpu.make_async_remote_copy(
            src_ref=gate_in_ref.at[row],
            dst_ref=gate_in_ref.at[row + place_of(step)[1]],
            send_sem=gate_fwd_send.at[step],
            recv_sem=gate_fwd_recv.at[step],
            device_id=sibling,
            device_id_type=MESH,
        )

    def slope_copy(step):
        return pltpu.make_async_remote_copy(
            src_ref=slope_out_ref.at[step],
            dst_ref=slope_in_ref.at[step],
            send_sem=slope_send.at[step],
            recv_sem=slope_recv.at[step],
            device_id={"expert": source(step)},
            device_id_type=MESH,
        )

    def pair_copy(part):
        start, count = parts[part]
        return pltpu.make_async_remote_copy(
            src_ref=part_ref.at[pl.ds((2 * start + count) * slots, count * slots)],
            dst_ref=pair_ref.at[pl.ds(start * slots, count * slots)],
            send_sem=pair_send.at[part],
            recv_sem=pair_recv.at[part],
            device_id=sibling,
            device_id_type=MESH,
        )

    def ret_copy(step):
        return pltpu.make_async_remote_copy(
            src_ref=ret_ref.at[pl.ds(step * slots, slots)],
            dst_ref=back_ref.at[pl.ds(step * slots, slots)],
            send_sem=ret_send.at[step],
            recv_sem=ret_recv.at[step],
            device_id={"expert": source(step)},
            device_id_type=MESH,
        )

    probs = table_ref[:, :tok_dev]
    probs_half = probs.astype(jnp.bfloat16)
    rank_gap = lax.broadcasted_iota(jnp.int32, (slots, capacity), 1) - lax.broadcasted_iota(
        jnp.int32, (slots, capacity), 0
    )
    rank_gap = rank_gap.astype(jnp.float32)
    token_id = lax.broadcasted_iota(jnp.int32, (tok_dev, capacity), 0) + base
    token_id = token_id.astype(jnp.float32)
    first_token = token_id[:1, :]
    expert_row = lax.broadcasted_iota(jnp.int32, (experts, chunk), 0)
    slot_gap = lax.broadcasted_iota(jnp.int32, (slots, chunk), 1) - lax.broadcasted_iota(
        jnp.int32, (slots, chunk), 0
    )

    def select(part):
        for step in range(part * half, (part + 1) * half):
            row = table_ref[pl.ds(target(step), 1), tok_dev + width :]
            before = jnp.sum(jnp.where(row < first_token, 1.0, 0.0), axis=1, keepdims=True)
            pick = jnp.where(rank_gap == before, 1.0, 0.0).astype(jnp.bfloat16)
            equal = jnp.where(token_id == row, 1.0, 0.0).astype(jnp.bfloat16)
            select_ref[pl.ds(step * slots, slots), :] = matmul(pick, equal, NT).astype(jnp.bfloat16)
        chosen = select_ref[pl.ds(part * chunk, chunk), :]
        both_rows = matmul(chosen, tokens_ref[...], NN).astype(jnp.bfloat16)
        gates = matmul(probs_half, chosen, NT)
        for index in range(half):
            step = part * half + index
            mine = slice(index * slots, (index + 1) * slots)
            gate = jnp.sum(
                jnp.where(expert_row == target(step), gates, 0.0), axis=0, keepdims=True
            )
            gate_ref = gate_out_ref if step else gate_in_ref
            gate_ref[step] = gate
            ref = rows_ref if step == 0 else send_ref
            at = pl.ds(step * slots, slots)
            ref[at, :] = both_rows[mine]

    select(1)
    pl.semaphore_wait(barrier, experts)
    for step in range(half, sum(parts[1])):
        go_copy(step).start()
        gate_copy(step).start()
    select(0)
    for step in range(1, half):
        go_copy(step).start()
        gate_copy(step).start()
    for step in range(parts[2][0], experts):
        go_copy(step).start()
        gate_copy(step).start()

    def forward(part):
        for step in range(parts[part][0], sum(parts[part])):
            if step:
                go_copy(step).wait_recv()
                gate_copy(step).wait_recv()
            fwd_copy(step).start()
            gate_fwd_copy(step).start()

    def compute(part):
        start, count = parts[part]
        for step in range(start, start + count):
            fwd_copy(step).wait_recv()
            gate_fwd_copy(step).wait_recv()
        rows = pl.ds(2 * start * slots, 2 * count * slots)
        blocks = []
        for index in range(2 * count):
            shift = ((start + index % count) % half) * slots
            row = jnp.broadcast_to(gate_in_ref[2 * start + index], (slots, chunk))
            blocks.append(
                jnp.sum(jnp.where(slot_gap == shift, row, 0.0), axis=1, keepdims=True)
            )
        gate = jnp.broadcast_to(jnp.concatenate(blocks, axis=0), (2 * count * slots, 128))
        wide_gate = jnp.concatenate([gate] * (width // 128), axis=1)
        scaled_ref[rows, :] = (
            wide_gate * rows_ref[rows, width : 2 * width].astype(jnp.float32)
        ).astype(jnp.bfloat16)
        part_ref[rows, :] = jnp.zeros((2 * count * slots, width + 128), jnp.float32)

        def step_tile(index, carry):
            at = pl.ds(pl.multiple_of(index * tile, tile), tile)
            w_first = w_in_ref[:, at]
            w_second = w_out_t_ref[:, at]
            pre_act = matmul(rows_ref[rows, :width], w_first, NN)
            raw_grad = matmul(rows_ref[rows, width : 2 * width], w_second, NN)
            gelu_value, gelu_slope = gelu_parts(pre_act)
            act = gelu_value.astype(jnp.bfloat16)
            act_ref[rows, at] = act
            product = act.astype(jnp.float32) * raw_grad
            gate_tile = jnp.concatenate([gate] * (tile // 128), axis=1)
            pre_grad = (gate_tile * raw_grad * gelu_slope).astype(jnp.bfloat16)
            pre_grad_ref[rows, at] = pre_grad
            part_ref[rows, :width] += matmul(pre_grad, w_in_t_ref[at, :], NN)
            total = product[:, :128]
            for lane in range(128, tile, 128):
                total = total + product[:, lane : lane + 128]
            part_ref[rows, width:] += total
            return carry

        lax.fori_loop(0, hidden // tile, step_tile, 0)
        pair_copy(part).start()

    def give_back(part):
        pair_copy(part).wait_recv()
        start, count = parts[part]
        own = part_ref[pl.ds(2 * start * slots, count * slots), :]
        total = own + pair_ref[pl.ds(start * slots, count * slots), :]
        gate_grad = jnp.sum(total[:, width:], axis=1, keepdims=True)
        values = total[:, :width].astype(jnp.bfloat16)
        for index in range(count):
            step = start + index
            mine = slice(index * slots, (index + 1) * slots)
            ref = ret_ref if step else back_ref
            ref[pl.ds(step * slots, slots), :] = values[mine]
            spread = jnp.broadcast_to(gate_grad[mine], (slots, chunk))
            slope_ref = slope_out_ref if step else slope_in_ref
            slope_ref[step] = jnp.sum(
                jnp.where(slot_gap == (step % half) * slots, spread, 0.0), axis=0, keepdims=True
            )
            if step:
                ret_copy(step).start()
                slope_copy(step).start()

    first_rows = 256
    second_rows = 256

    def first_grad(index, carry):
        at = pl.ds(pl.multiple_of(index * first_rows, first_rows), first_rows)
        first_ref[0, at, :] = matmul(rows_ref[:, at], pre_grad_ref[...], TN).astype(jnp.bfloat16)
        return carry

    def second_grad(index, carry):
        at = pl.ds(pl.multiple_of(index * second_rows, second_rows), second_rows)
        second_ref[0, at, :] = matmul(act_ref[:, at], scaled_ref[...], TN).astype(jnp.bfloat16)
        return carry

    first_count = width // first_rows
    second_count = hidden // second_rows
    for load in loads:
        load.wait()

    def turn(index, carry):
        at = pl.ds(pl.multiple_of(index * 256, 256), 256)
        w_in_t_ref[at, :] = w_in_ref[:, at].T
        w_out_t_ref[:, at] = w_out_ref[at, :].T
        return carry

    lax.fori_loop(0, hidden // 256, turn, 0)
    forward(0)
    compute(0)
    forward(1)
    give_back(0)
    compute(1)
    forward(2)
    give_back(1)
    compute(2)
    lax.fori_loop(0, 1, first_grad, 0)
    give_back(2)
    lax.fori_loop(1, first_count, first_grad, 0)
    lax.fori_loop(0, second_count, second_grad, 0)

    def collect(start, stop):
        for step in range(max(start, 1), stop):
            ret_copy(step).wait_recv()
            slope_copy(step).wait_recv()
        rows = pl.ds(start * slots, (stop - start) * slots)
        coded = jnp.zeros((experts, chunk), jnp.float32)
        for step in range(start, stop):
            coded += jnp.where(expert_row == target(step), slope_in_ref[step], 0.0)
        high = coded.astype(jnp.bfloat16)
        low = (coded - high.astype(jnp.float32)).astype(jnp.bfloat16)
        chosen = select_ref[rows, :]
        scores = matmul(high, chosen, NN) + matmul(low, chosen, NN)
        return matmul(chosen, back_ref[rows, :], TN), scores

    early_grad, early_scores = collect(0, half)
    late_grad, late_scores = collect(half, experts)
    score_grad = early_scores + late_scores
    grad_logits = probs * (score_grad - jnp.sum(probs * score_grad, axis=0, keepdims=True))
    grad_logits_ref[...] = grad_logits
    router_part = lax.dot_general(
        grad_logits,
        table_ref[:, tok_dev : tok_dev + width],
        (TN, ((), ())),
        precision=lax.Precision.HIGHEST,
        preferred_element_type=jnp.float32,
    )
    grad_tokens_ref[...] = (early_grad + late_grad + router_part).astype(jnp.bfloat16)

    for step in range(1, experts):
        go_copy(step).wait_send()
        gate_copy(step).wait_send()
        ret_copy(step).wait_send()
        slope_copy(step).wait_send()
    for step in range(experts):
        fwd_copy(step).wait_send()
        gate_fwd_copy(step).wait_send()
    for part in range(len(parts)):
        pair_copy(part).wait_send()


def write_kernel(*refs):
    count = len(refs) // 2
    copies = [
        pltpu.make_async_copy(refs[index], refs[count + index], refs[-1].at[index])
        for index in range(count)
    ]
    for copy in copies:
        copy.start()
    for copy in copies:
        copy.wait()


def fused_body(tokens, grad_out, probs, choices, w_in, w_out, router):
    tok_dev, width = tokens.shape
    experts, capacity = choices.shape
    hidden = w_in.shape[2]
    slots = 2 * capacity // (experts * lax.axis_size("hidden"))
    total = experts * slots
    half_type = jnp.bfloat16
    vmem = pl.BlockSpec(memory_space=pltpu.VMEM)
    hbm = pl.BlockSpec(memory_space=pltpu.HBM)
    dma = pltpu.SemaphoreType.DMA
    shapes = (
        jax.ShapeDtypeStruct(tokens.shape, half_type),
        jax.ShapeDtypeStruct(probs.shape[::-1], jnp.float32),
        jax.ShapeDtypeStruct(w_in.shape, half_type),
        jax.ShapeDtypeStruct(w_out.shape, half_type),
    )
    stacked = jnp.concatenate([tokens, grad_out], axis=1)
    table = jnp.concatenate([probs.T, router.T, choices.astype(jnp.float32)], axis=1)
    held = pl.pallas_call(
        functools.partial(fused_kernel, experts, slots, 512),
        out_shape=shapes,
        in_specs=[vmem, vmem, hbm, hbm],
        out_specs=(vmem,) * 4,
        scratch_shapes=[
            pltpu.VMEM((width, hidden), half_type),
            pltpu.VMEM((hidden, width), half_type),
            pltpu.VMEM((hidden, width), half_type),
            pltpu.VMEM((width, hidden), half_type),
            pltpu.VMEM((total, tok_dev), half_type),
            pltpu.VMEM((total, 2 * width), half_type),
            pltpu.VMEM((2 * total, 2 * width), half_type),
            pltpu.VMEM((2 * total, width), half_type),
            pltpu.VMEM((2 * total, hidden), half_type),
            pltpu.VMEM((2 * total, hidden), half_type),
            pltpu.VMEM((2 * total, width + 128), jnp.float32),
            pltpu.VMEM((total, width + 128), jnp.float32),
            pltpu.VMEM((total, width), half_type),
            pltpu.VMEM((total, width), half_type),
            pltpu.VMEM((experts, 1, 128), jnp.float32),
            pltpu.VMEM((2 * experts, 1, 128), jnp.float32),
            pltpu.VMEM((experts, 1, 128), jnp.float32),
            pltpu.VMEM((experts, 1, 128), jnp.float32),
            dma((2,)),
            dma((experts,)),
            dma((experts,)),
            dma((experts,)),
            dma((experts,)),
            dma((3,)),
            dma((3,)),
            dma((experts,)),
            dma((experts,)),
        ]
        + [dma((experts,))] * 6,
        compiler_params=pltpu.CompilerParams(
            collective_id=0, has_side_effects=True, vmem_limit_bytes=48 * 1024 * 1024
        ),
        cost_estimate=pl.CostEstimate(
            flops=20 * total * width * hidden,
            bytes_accessed=8 * width * hidden,
            transcendentals=2 * total * hidden,
        ),
    )(stacked, table, w_in, w_out)
    grad_tokens, grad_logits, grad_w_in, grad_w_out = pl.pallas_call(
        write_kernel,
        out_shape=shapes,
        in_specs=[pl.BlockSpec(memory_space=pl.ANY)] * 4,
        out_specs=(hbm,) * 4,
        scratch_shapes=[dma((4,))],
        compiler_params=pltpu.CompilerParams(vmem_limit_bytes=1024 * 1024),
    )(*held)
    return (grad_tokens, grad_w_in, grad_w_out, grad_logits.T)


def body(tokens, grad_out, probs, choices, w_in, w_out, router):
    experts, capacity = choices.shape
    owners = experts * lax.axis_size("hidden")
    slots = 2 * capacity // owners
    fits = (
        lax.axis_size("hidden") == 2
        and experts % 4 == 0
        and slots % 16 == 0
        and tokens.shape[0] % 128 == 0
        and experts * slots == 256
        and w_in.shape[0] == 1
        and 2 * experts <= 128
        and w_in.shape[1] % 256 == 0
        and w_in.shape[2] % 512 == 0
    )
    chosen = fused_body if fits else general_body
    return chosen(tokens, grad_out, probs, choices, w_in, w_out, router)


def solution(mesh):
    in_specs = (
        P(("groups", "expert", "hidden"), None),
        P(("groups", "expert", "hidden"), None),
        P(("groups", "expert", "hidden"), None),
        P("groups", None),
        P("expert", None, "hidden"),
        P("expert", "hidden", None),
        P(),
    )
    out_specs = (
        P(("groups", "expert", "hidden"), None),
        P(("groups", "expert"), None, "hidden"),
        P(("groups", "expert"), "hidden", None),
        P(("groups", "expert", "hidden"), None),
    )
    return jax.shard_map(body, mesh=mesh, in_specs=in_specs, out_specs=out_specs, check_vma=False)
```
